256 devices in a mesh: lib: 32 (over z, x_lo, core), ref: 8 (over y, x_hi).
Axes of the slice: x: 4 (x_hi: 2, x_lo: 2; x = x_hi * 2 + x_lo), y: 4, z: 8, core: 2. Of those that a mesh axis runs over, the one named last changes fastest.
Arguments:
- compounds: bfloat16 [262144, 512], P(('lib', 'ref')), may hold values from 0 to 2.5, as said below
- compound_weight: float32 [262144], P(('lib', 'ref')), may hold values from 0.5 to 12, as said below
- reference_prints: bfloat16 [4096, 512], P('ref'), may hold values from 0 to 2.5, as said below
- potency: bfloat16 [4096], P('ref'), may hold values from 4 to 10
- target_label: int32 [4096], P('ref'), may hold values from 0 to 255, as said below
Outputs:
- whitened: float32 [262144, 256], P(('lib', 'ref'))
The draws below stay inside these ranges and needn't reach their ends.
Inputs may be any that keep to these rules, and one draw needn't show every extreme that they name: `target_label`: each of the 256 targets labels exactly 16 actives. `compounds`: nonnegative; every row has an entry of 0.25 or more. `reference_prints`: nonnegative; every row has an entry of 0.25 or more. `compound_weight`: positive.
All inputs are finite; a program needn't handle non-finite values.
Results may differ from the reference program's by a relative error of at most 0.0015.
Values may be sent and summed in bfloat16 or wider, within the bound.
No kernel may reach another device: no remote copies, remote signals or barrier semaphores. Data moves between devices by JAX's collectives and lax.ppermute only.
A program may use at most 64 MiB of HBM per device.

```python
import math
import jax
import jax.numpy as jnp
from jax import lax

BITS = 512
TARGETS = 256
COMPOUNDS = 262144
REFS = 4096


def fingerprint(key, count, width, low, high):
    key_bits, key_strength = jax.random.split(key)
    present = jax.random.uniform(key_bits, (count, width), dtype=jnp.float32) < 0.35
    strength = jax.random.uniform(key_strength, (count, width), dtype=jnp.float32, minval=low, maxval=high)
    forced = jnp.arange(width)[None, :] == jnp.arange(count)[:, None] % width
    return jnp.where(present | forced, strength, 0.0)


def base_references(key):
    return fingerprint(jax.random.fold_in(key, 101), REFS, BITS, 0.5, 2.0)


def draw_reference_prints(key, part):
    shared = base_references(key)
    return shared.astype(jnp.bfloat16)


def draw_compounds(key, part):
    key = jax.random.fold_in(key, 2)
    key_own = jax.random.fold_in(key, 0)
    own = fingerprint(key_own, COMPOUNDS, BITS, 0.5, 2.0)
    return own.astype(jnp.bfloat16)


def draw_target_label(key, part):
    key = jax.random.fold_in(key, 3)
    return (jax.random.permutation(key, REFS) % TARGETS).astype(jnp.int32)


def draw_compound_weight(key, part):
    key = jax.random.fold_in(key, 4)
    position = jnp.arange(COMPOUNDS, dtype=jnp.float32) / max(COMPOUNDS - 1, 1)
    jitter = jax.random.uniform(key, (COMPOUNDS,), dtype=jnp.float32, minval=0.6, maxval=1.4)
    return jnp.exp(math.log(3.0) * position) * jitter


def level_of(rng, dims, cuts, least, largest):
    level, own = 1.0, jax.random.fold_in(rng, 6)
    for dim, shards_of in cuts:
        draws = jnp.exp(jax.random.uniform(jax.random.fold_in(own, dim), (shards_of,), jnp.float32, least / len(cuts), largest / len(cuts)))
        level = level * jnp.repeat(draws, dims[dim] // shards_of).reshape([-1 if axis == dim else 1 for axis in range(len(dims))])
    return level


def setup_inputs(seed: int = 0) -> dict:
    splits = jax.random.split(jax.random.key(seed), 6)
    compounds = draw_compounds(jax.random.fold_in(splits[5], 71), 0)
    compound_weight = draw_compound_weight(jax.random.fold_in(splits[5], 71), 0)
    reference_prints = draw_reference_prints(jax.random.fold_in(splits[5], 71), 0)
    potency = jnp.clip(4.0 + 6.0 * jax.random.uniform(splits[3], (REFS,), jnp.float32) ** level_of(splits[3], (REFS,), ((0, 8),), -0.2, 0.2), 4.0, 10.0).astype(jnp.bfloat16)
    target_label = draw_target_label(jax.random.fold_in(splits[5], 71), 0)
    return dict(compounds=compounds, compound_weight=compound_weight, reference_prints=reference_prints, potency=potency, target_label=target_label)


SHARPNESS = 320.0
SHRINKAGE = 0.02

def reference(compounds, compound_weight, reference_prints, potency, target_label):
    ref_norm = lax.optimization_barrier(jnp.sum(reference_prints.astype(jnp.float32) ** 2, axis=1))
    columns = jnp.arange(TARGETS, dtype=jnp.int32)
    values = (target_label[:, None] == columns[None, :]).astype(jnp.bfloat16) * potency[:, None]
    block_rows = math.gcd(COMPOUNDS, 512)
    blocks = compounds.reshape(COMPOUNDS // block_rows, block_rows, BITS)

    def profile_block(block):
        query_norm = lax.optimization_barrier(jnp.sum(block.astype(jnp.float32) ** 2, axis=1))
        intersection = jnp.dot(block.astype(jnp.float32), reference_prints.T.astype(jnp.float32), preferred_element_type=jnp.float32)
        scores = SHARPNESS * intersection / (query_norm[:, None] + ref_norm[None, :] - intersection)
        row_top = lax.optimization_barrier(jnp.max(scores, axis=1, keepdims=True))
        expo = jnp.exp(scores - row_top).astype(jnp.bfloat16)
        denominator = lax.optimization_barrier(jnp.sum(expo.astype(jnp.float32), axis=1))
        numerator = jnp.dot(expo.astype(jnp.float32), values.astype(jnp.float32), preferred_element_type=jnp.float32)
        return numerator / denominator[:, None]
    profile = lax.map(profile_block, blocks).reshape(COMPOUNDS, TARGETS)
    weight_total = jnp.sum(compound_weight)
    average = jnp.dot(compound_weight, profile, precision=lax.Precision.HIGHEST) / weight_total
    centered = profile - average[None, :]
    covariance = jnp.dot(centered.T, compound_weight[:, None] * centered, precision=lax.Precision.HIGHEST) / weight_total
    covariance = covariance + SHRINKAGE * jnp.eye(TARGETS, dtype=jnp.float32)
    factor = lax.linalg.cholesky(covariance)
    solved = lax.linalg.triangular_solve(factor, centered.T, left_side=True, lower=True)
    return solved.T * jnp.sqrt(compound_weight)[:, None]
```

```python
import functools

import jax
import jax.numpy as jnp
from jax import lax
from jax.experimental import pallas as pl
from jax.experimental.pallas import tpu as pltpu
from jax.sharding import PartitionSpec as P

ALL = ("lib", "ref")
BITS = 512
EXTRA = 16
DEPTH = BITS + EXTRA
TARGETS = 256
SHRINKAGE = 0.02
LOG2E = 1.4426950408889634
SCALE = 320.0 * LOG2E
MARGIN = 58.0
BLOCK = 256
PANEL = 32
F32 = jnp.float32
BF16 = jnp.bfloat16
EXACT = lax.Precision.HIGHEST
VMEM = pl.BlockSpec(memory_space=pltpu.VMEM)


def params(mib=40):
    return pltpu.CompilerParams(vmem_limit_bytes=mib * 2**20)


def cost(flops, size):
    return pl.CostEstimate(flops=flops, bytes_accessed=size, transcendentals=0)


def place(x, y, z, c):
    return ((z % 8 * 2 + x % 2) * 2 + c % 2) * 8 + y % 4 * 2 + x // 2


def route(move):
    pairs = []
    for x in range(4):
        for y in range(4):
            for z in range(8):
                for c in range(2):
                    pairs.append((place(x, y, z, c), place(*move(x, y, z, c))))
    return sorted(pairs)


def send(value, move):
    return lax.ppermute(value, ALL, route(move))


def up(x, y, z, c):
    return x, y + 1, z, c


def down(x, y, z, c):
    return x, y - 1, z, c


def flip(x, y, z, c):
    return 3 - x, y, z, c


def sibling(x, y, z, c):
    return x, y, z, 1 - c


def prep_kernel(core_ref, prints_ref, potency_ref, label_ref, whole_ref, half_ref):
    prints = prints_ref[...].T
    wide = prints.astype(F32)
    norm = jnp.sum(wide * wide, axis=0, keepdims=True)
    high = norm.astype(BF16)
    rest = norm - high.astype(F32)
    middle = rest.astype(BF16)
    low = (rest - middle.astype(F32)).astype(BF16)
    row = lax.broadcasted_iota(jnp.int32, (EXTRA, prints.shape[1]), 0)
    extra = jnp.where(row == 0, potency_ref[...].astype(F32), 0.0)
    extra = jnp.where(row == 1, label_ref[...].astype(F32), extra)
    for at, part in ((2, high), (3, middle), (4, low)):
        extra = jnp.where(row == at, part.astype(F32), extra)
    extra = extra.astype(BF16)
    whole_ref[:BITS, :] = prints
    whole_ref[BITS:, :] = extra
    first = core_ref[0] == 0
    half = prints.shape[1] // 2

    @pl.when(first)
    def _():
        half_ref[:BITS, :] = prints[:, :half]
        half_ref[BITS:, :] = extra[:, :half]

    @pl.when(jnp.logical_not(first))
    def _():
        half_ref[:BITS, :] = prints[:, half:]
        half_ref[BITS:, :] = extra[:, half:]


def prepare(core, prints, potency, label):
    refs = prints.shape[0]
    return pl.pallas_call(
        prep_kernel,
        in_specs=[pl.BlockSpec(memory_space=pltpu.SMEM), VMEM, VMEM, VMEM],
        out_specs=[VMEM, VMEM],
        out_shape=[
            jax.ShapeDtypeStruct((DEPTH, refs), BF16),
            jax.ShapeDtypeStruct((DEPTH, refs // 2), BF16),
        ],
        compiler_params=params(),
        name="prepare",
    )(core, prints, potency, label)


def piece_scores(queries, query_norm, piece_ref):
    extra = piece_ref[BITS:, :].astype(F32)
    norm = extra[2:3] + extra[3:4] + extra[4:5]
    inter = jnp.dot(queries, piece_ref[:BITS, :], preferred_element_type=F32)
    inverse = 1.0 / ((query_norm + norm) - inter)
    return (inter * inverse) * SCALE


def piece_values(piece_ref):
    extra = piece_ref[BITS:, :].astype(F32)
    target = lax.broadcasted_iota(jnp.int32, (TARGETS, extra.shape[1]), 0)
    hit = target == extra[1:2].astype(jnp.int32)
    return jnp.where(hit, extra[0:1], 0.0).astype(BF16)


def add_piece(scores, top, piece_ref, num, den):
    expo = jnp.exp2(scores - top).astype(BF16)
    rounded = expo.astype(F32)
    for k in range(expo.shape[1] // 128):
        den = den + rounded[:, k * 128 : (k + 1) * 128]
    num = num + lax.dot_general(
        expo,
        piece_values(piece_ref),
        (((1,), (1,)), ((), ())),
        preferred_element_type=F32,
    )
    return num, den


def squared_norm(queries):
    wide = queries.astype(F32)
    return jnp.sum(wide * wide, axis=1, keepdims=True)


def first_kernel(queries_ref, piece_ref, num_ref, den_ref, top_ref):
    queries = queries_ref[...]
    rows = queries.shape[0]
    scores = piece_scores(queries, squared_norm(queries), piece_ref)
    top = jnp.max(scores, axis=1, keepdims=True) + MARGIN
    num = jnp.zeros((rows, TARGETS), F32)
    den = jnp.zeros((rows, 128), F32)
    num, den = add_piece(scores, top, piece_ref, num, den)
    num_ref[...] = num
    den_ref[...] = den
    top_ref[...] = jnp.broadcast_to(top, (rows, 128))


def more_kernel(count, *refs):
    queries_ref, num_in, den_in, top_ref = refs[:4]
    pieces = refs[4 : 4 + count]
    num_ref, den_ref = refs[4 + count :]
    queries = queries_ref[...]
    query_norm = squared_norm(queries)
    top = top_ref[:, 0:1]
    num, den = num_in[...], den_in[...]
    for piece_ref in pieces:
        scores = piece_scores(queries, query_norm, piece_ref)
        num, den = add_piece(scores, top, piece_ref, num, den)
    num_ref[...] = num
    den_ref[...] = den


def last_kernel(count, past, *refs):
    queries_ref, num_in, den_in, top_ref, weight_ref = refs[:5]
    pieces = refs[5 : 5 + count]
    earlier = refs[5 + count : 5 + count + past]
    profile_ref, moments_ref = refs[5 + count + past : 7 + count + past]
    buffers = refs[7 + count + past : -1]
    done = refs[-1]
    step = pl.program_id(0)
    rows = queries_ref.shape[0]
    queries = queries_ref[...]
    query_norm = squared_norm(queries)
    top = top_ref[:, 0:1]
    num, den = num_in[...], den_in[...]
    for piece_ref in pieces:
        scores = piece_scores(queries, query_norm, piece_ref)
        num, den = add_piece(scores, top, piece_ref, num, den)
    total = jnp.sum(den, axis=1, keepdims=True)
    here = pl.ds(pl.multiple_of(step * rows, rows), rows)
    profile_ref[here, :] = num * (1.0 / total)

    @pl.when(jnp.logical_not(jnp.max(total) <= 1.0))
    def _():
        copies = [
            pltpu.make_async_copy(source, buffer, done.at[k])
            for k, (source, buffer) in enumerate(zip(earlier, buffers))
        ]
        for copy in copies:
            copy.start()
        for copy in copies:
            copy.wait()
        everything = list(pieces) + list(buffers)
        best = jnp.full((rows, 1), -1.0, F32)
        for piece_ref in everything:
            scores = piece_scores(queries, query_norm, piece_ref)
            best = jnp.maximum(best, jnp.max(scores, axis=1, keepdims=True))
        again = jnp.zeros((rows, TARGETS), F32)
        weight = jnp.zeros((rows, 128), F32)
        for piece_ref in everything:
            scores = piece_scores(queries, query_norm, piece_ref)
            again, weight = add_piece(scores, best, piece_ref, again, weight)
        profile_ref[here, :] = again * (1.0 / jnp.sum(weight, axis=1, keepdims=True))

    @pl.when(step == pl.num_programs(0) - 1)
    def _():
        profile = profile_ref[...]
        weight = weight_ref[...]
        weight_total = jnp.sum(weight, axis=0, keepdims=True)
        first = jnp.sum(profile * weight, axis=0, keepdims=True)
        mean = first / weight_total
        spread = (profile - mean) * jnp.sqrt(weight)
        outer = (((0,), (0,)), ((), ()))
        moments = lax.dot_general(
            spread, spread, outer, precision=EXACT, preferred_element_type=F32
        ) + lax.dot_general(mean, first, outer, precision=EXACT, preferred_element_type=F32)
        row = lax.broadcasted_iota(jnp.int32, (TARGETS, TARGETS), 0)
        column = lax.broadcasted_iota(jnp.int32, (TARGETS, TARGETS), 1)
        moments = jnp.where((row == 0) & (column > 0), first, moments)
        moments = jnp.where((row == 1) & (column == 2), first[0:1, 0:1], moments)
        moments = jnp.where((row == 1) & (column == 3), weight_total, moments)
        moments_ref[...] = moments


def state_specs():
    return [
        pl.BlockSpec((BLOCK, BITS), lambda i: (i, 0)),
        pl.BlockSpec((BLOCK, TARGETS), lambda i: (i, 0)),
        pl.BlockSpec((BLOCK, 128), lambda i: (i, 0)),
        pl.BlockSpec((BLOCK, 128), lambda i: (i, 0)),
    ]


def whole(array):
    zeros = (0,) * array.ndim
    return pl.BlockSpec(array.shape, lambda i: zeros)


def work(rows, pieces):
    refs = sum(piece.shape[1] for piece in pieces)
    return cost(6 * rows * refs * (BITS + TARGETS), rows * 2048 + refs * DEPTH * 2)


def first_part(queries, piece):
    rows = queries.shape[0]
    specs = state_specs()
    return pl.pallas_call(
        first_kernel,
        grid=(rows // BLOCK,),
        in_specs=[specs[0], whole(piece)],
        out_specs=specs[1:],
        out_shape=[
            jax.ShapeDtypeStruct((rows, TARGETS), F32),
            jax.ShapeDtypeStruct((rows, 128), F32),
            jax.ShapeDtypeStruct((rows, 128), F32),
        ],
        compiler_params=params(),
        cost_estimate=work(rows, [piece]),
        name="first_part",
    )(queries, piece)


def more_part(queries, state, pieces):
    rows = queries.shape[0]
    specs = state_specs()
    num, den = pl.pallas_call(
        functools.partial(more_kernel, len(pieces)),
        grid=(rows // BLOCK,),
        in_specs=specs + [whole(piece) for piece in pieces],
        out_specs=specs[1:3],
        out_shape=[
            jax.ShapeDtypeStruct((rows, TARGETS), F32),
            jax.ShapeDtypeStruct((rows, 128), F32),
        ],
        compiler_params=params(),
        cost_estimate=work(rows, pieces),
        name="more_part",
    )(queries, *state, *pieces)
    return num, den, state[2]


def last_part(queries, state, weight, pieces, earlier):
    rows = queries.shape[0]
    return pl.pallas_call(
        functools.partial(last_kernel, len(pieces), len(earlier)),
        grid=(rows // BLOCK,),
        in_specs=state_specs()
        + [whole(weight)]
        + [whole(piece) for piece in pieces]
        + [pl.BlockSpec(memory_space=pl.ANY)] * len(earlier),
        out_specs=[
            pl.BlockSpec((rows, TARGETS), lambda i: (0, 0)),
            pl.BlockSpec((TARGETS, TARGETS), lambda i: (0, 0)),
        ],
        out_shape=[
            jax.ShapeDtypeStruct((rows, TARGETS), F32),
            jax.ShapeDtypeStruct((TARGETS, TARGETS), F32),
        ],
        scratch_shapes=[pltpu.VMEM(piece.shape, BF16) for piece in earlier]
        + [pltpu.SemaphoreType.DMA((len(earlier),))],
        compiler_params=params(),
        cost_estimate=work(rows, pieces),
        name="last_part",
    )(queries, *state, weight, *pieces, *earlier)


def repeat_row(block, at):
    return jnp.broadcast_to(block[at : at + 1, :], block.shape)


def inverse_factor(schur, size):
    groups = PANEL // 8
    panels = size // PANEL
    sub = lax.broadcasted_iota(jnp.int32, (8, 128), 0)
    eye = (
        lax.broadcasted_iota(jnp.int32, (PANEL, PANEL), 0)
        == lax.broadcasted_iota(jnp.int32, (PANEL, PANEL), 1)
    ).astype(F32)
    schur = [schur[i * PANEL : (i + 1) * PANEL, :] for i in range(panels)]
    inverse = [None] * panels
    result = []
    for t in range(panels):
        start = t * PANEL
        lane0 = start // 128 * 128
        left = schur[t][:, lane0:]
        right = [inverse[t]] if t else []
        right.append(eye)
        width = start + PANEL
        if width % 128:
            right.append(jnp.zeros((PANEL, -width % 128), F32))
        right = jnp.concatenate(right, axis=1)
        nl, nr = left.shape[1] // 128, right.shape[1] // 128
        tiles = [
            [left[8 * g : 8 * g + 8, 128 * k : 128 * k + 128] for k in range(nl)]
            + [right[8 * g : 8 * g + 8, 128 * k : 128 * k + 128] for k in range(nr)]
            for g in range(groups)
        ]
        square = left[:, start - lane0 : start - lane0 + PANEL]
        spread = [
            [
                jnp.broadcast_to(square[8 * g : 8 * g + 8, k : k + 1], (8, 128))
                if g >= k // 8
                else None
                for g in range(groups)
            ]
            for k in range(PANEL)
        ]
        inverses = []
        for k in range(PANEL):
            own, at = divmod(k, 8)
            inv = 1.0 / repeat_row(spread[k][own], at)
            inverses.append(inv)
            column = [
                spread[k][g] if g > own else jnp.where(sub > at, spread[k][g], 0.0) if g == own else None
                for g in range(groups)
            ]
            for m in range(k + 1, PANEL):
                factor = repeat_row(spread[k][m // 8], m % 8)
                for g in range(m // 8, groups):
                    spread[m][g] = spread[m][g] - (column[g] * factor) * inv
            multiple = [None if c is None else c * inv for c in column]
            for k2 in range(nl + nr):
                row = repeat_row(tiles[own][k2], at)
                for g in range(own, groups):
                    tiles[g][k2] = tiles[g][k2] - multiple[g] * row
        scale = []
        for g in range(groups):
            column = inverses[8 * g]
            for o in range(1, 8):
                column = jnp.where(sub == o, inverses[8 * g + o], column)
            scale.append(column)
        root = [jnp.sqrt(column) for column in scale]
        blank = [jnp.zeros((8, 128), F32)] * (size // 128 - nr)
        result.append(
            jnp.concatenate(
                [
                    jnp.concatenate([tiles[g][nl + k] * root[g] for k in range(nr)] + blank, axis=1)
                    for g in range(groups)
                ],
                axis=0,
            )
        )
        if t == panels - 1:
            break
        upper = jnp.concatenate([jnp.concatenate(tiles[g], axis=1) for g in range(groups)], axis=0)
        scaled = jnp.concatenate(
            [
                jnp.concatenate([tiles[g][k] * scale[g] for k in range(nl)], axis=1)
                for g in range(groups)
            ],
            axis=0,
        )
        for low, high in ((t + 1, t + 2), (t + 2, panels)):
            if low >= high:
                continue
            update = lax.dot_general(
                scaled[:, low * PANEL - lane0 : high * PANEL - lane0],
                upper,
                (((0,), (0,)), ((), ())),
                precision=EXACT,
                preferred_element_type=F32,
            )
            for i in range(low, high):
                part = update[(i - low) * PANEL : (i - low + 1) * PANEL]
                kept = [schur[i][:, :lane0]] if lane0 else []
                schur[i] = jnp.concatenate(kept + [schur[i][:, lane0:] - part[:, : nl * 128]], axis=1)
                fresh = -part[:, nl * 128 : nl * 128 + width]
                if inverse[i] is not None:
                    fresh = jnp.concatenate([inverse[i] + fresh[:, :start], fresh[:, start:]], axis=1)
                inverse[i] = fresh
    return jnp.concatenate(result, axis=0)


def whiten_kernel(moments_ref, profile_ref, weight_ref, out_ref):
    total = moments_ref[...]
    row = lax.broadcasted_iota(jnp.int32, (TARGETS, TARGETS), 0)
    column = lax.broadcasted_iota(jnp.int32, (TARGETS, TARGETS), 1)
    share = 1.0 / total[1:2, 3:4]
    first = jnp.where(column[0:1] == 0, total[1:2, 2:3], total[0:1, :])
    mean = first * share
    outer = lax.dot_general(
        mean, mean, (((0,), (0,)), ((), ())), precision=EXACT, preferred_element_type=F32
    )
    lower = jnp.where(column <= row, total, 0.0)
    strict = jnp.where(column < row, total, 0.0)
    covariance = (lower + strict.T) * share - outer
    covariance = covariance + jnp.where(row == column, SHRINKAGE, 0.0)
    inverse = inverse_factor(covariance, TARGETS)
    centered = (profile_ref[...] - mean) * jnp.sqrt(weight_ref[...])
    out_ref[...] = lax.dot_general(
        centered, inverse, (((1,), (1,)), ((), ())), precision=EXACT, preferred_element_type=F32
    )


def whiten(moments, profile, weight):
    return pl.pallas_call(
        whiten_kernel,
        in_specs=[VMEM, VMEM, VMEM],
        out_specs=VMEM,
        out_shape=jax.ShapeDtypeStruct(profile.shape, F32),
        compiler_params=params(),
        name="whiten",
    )(moments, profile, weight)


def on_device(compounds, compound_weight, reference_prints, potency, target_label):
    devices = lax.axis_size(ALL)
    core = lax.rem(lax.axis_index("lib"), 2).astype(jnp.int32).reshape(1)
    weight = compound_weight[:, None]
    own, half = prepare(core, reference_prints, potency[None, :], target_label[None, :])
    middle = half.shape[1] // 2

    flipped, above, below = send(half, flip), send(half, up), send(half, down)
    far_a = send(above[:, :middle], up)
    far_b = send(below[:, middle:], down)
    flipped_above, flipped_below = send(flipped, up), send(flipped, down)
    flipped_far_a = send(flipped_above[:, :middle], up)
    flipped_far_b = send(flipped_below[:, middle:], down)

    near = [flipped, above, below]
    near += [send(piece, sibling) for piece in near]
    later = [far_a, far_b, flipped_above, flipped_below, flipped_far_a, flipped_far_b]
    later += [send(piece, sibling) for piece in later]

    state = first_part(compounds, own)
    state = more_part(compounds, state, near)
    profile, moments = last_part(compounds, state, weight, later, [own] + near)

    shares = lax.all_to_all(moments.reshape(devices, 2, TARGETS // 2), ALL, 0, 0)
    share = jnp.sum(shares, axis=0, keepdims=True)
    total = lax.all_to_all(jnp.broadcast_to(share, shares.shape), ALL, 0, 0)
    return whiten(total.reshape(TARGETS, TARGETS), profile, weight)


def solution(mesh):
    placed = (P(("lib", "ref"), None), P(("lib", "ref")), P("ref", None), P("ref"), P("ref"))
    return jax.shard_map(
        on_device, mesh=mesh, in_specs=placed, out_specs=P(("lib", "ref"), None), check_vma=False
    )
```

```python
import functools

import jax
import jax.numpy as jnp
from jax import lax
from jax.experimental import pallas as pl
from jax.experimental.pallas import tpu as pltpu
from jax.sharding import PartitionSpec as P

ALL = ("lib", "ref")
BITS = 512
EXTRA = 16
DEPTH = BITS + EXTRA
TARGETS = 256
SHRINKAGE = 0.02
LOG2E = 1.4426950408889634
SCALE = 320.0 * LOG2E
MARGIN = 58.0
PANEL = 32
F32 = jnp.float32
BF16 = jnp.bfloat16
EXACT = lax.Precision.HIGHEST
VMEM = pl.BlockSpec(memory_space=pltpu.VMEM)


def params(mib=40):
    return pltpu.CompilerParams(vmem_limit_bytes=mib * 2**20)


def cost(flops, size):
    return pl.CostEstimate(flops=flops, bytes_accessed=size, transcendentals=0)


def place(x, y, z, c):
    return ((z % 8 * 2 + x % 2) * 2 + c % 2) * 8 + y % 4 * 2 + x // 2


def route(move):
    pairs = []
    for x in range(4):
        for y in range(4):
            for z in range(8):
                for c in range(2):
                    pairs.append((place(x, y, z, c), place(*move(x, y, z, c))))
    return sorted(pairs)


def send(value, move):
    return lax.ppermute(value, ALL, route(move))


def up(x, y, z, c):
    return x, y + 1, z, c


def down(x, y, z, c):
    return x, y - 1, z, c


def up2(x, y, z, c):
    return x, y + 2, z, c


def flip(x, y, z, c):
    return 3 - x, y, z, c


def sibling(x, y, z, c):
    return x, y, z, 1 - c


def prep_kernel(core_ref, prints_ref, potency_ref, label_ref, whole_ref, half_ref):
    prints = prints_ref[...].T
    wide = prints.astype(F32)
    norm = jnp.sum(wide * wide, axis=0, keepdims=True)
    high = norm.astype(BF16)
    rest = norm - high.astype(F32)
    middle = rest.astype(BF16)
    low = (rest - middle.astype(F32)).astype(BF16)
    row = lax.broadcasted_iota(jnp.int32, (EXTRA, prints.shape[1]), 0)
    extra = jnp.where(row == 0, potency_ref[...].astype(F32), 0.0)
    extra = jnp.where(row == 1, label_ref[...].astype(F32), extra)
    for at, part in ((2, high), (3, middle), (4, low)):
        extra = jnp.where(row == at, part.astype(F32), extra)
    extra = extra.astype(BF16)
    whole_ref[:BITS, :] = prints
    whole_ref[BITS:, :] = extra
    first = core_ref[0] == 0
    half = prints.shape[1] // 2

    @pl.when(first)
    def _():
        half_ref[:BITS, :] = prints[:, :half]
        half_ref[BITS:, :] = extra[:, :half]

    @pl.when(jnp.logical_not(first))
    def _():
        half_ref[:BITS, :] = prints[:, half:]
        half_ref[BITS:, :] = extra[:, half:]


def prepare(core, prints, potency, label):
    refs = prints.shape[0]
    return pl.pallas_call(
        prep_kernel,
        in_specs=[pl.BlockSpec(memory_space=pltpu.SMEM), VMEM, VMEM, VMEM],
        out_specs=[VMEM, VMEM],
        out_shape=[
            jax.ShapeDtypeStruct((DEPTH, refs), BF16),
            jax.ShapeDtypeStruct((DEPTH, refs // 2), BF16),
        ],
        compiler_params=params(),
        name="prepare",
    )(core, prints, potency, label)


def piece_scores(queries, query_norm, piece_ref):
    extra = piece_ref[BITS:, :].astype(F32)
    norm = extra[2:3] + extra[3:4] + extra[4:5]
    inter = jnp.dot(queries, piece_ref[:BITS, :], preferred_element_type=F32)
    inverse = 1.0 / ((query_norm + norm) - inter)
    return (inter * inverse) * SCALE


def piece_values(piece_ref):
    extra = piece_ref[BITS:, :].astype(F32)
    target = lax.broadcasted_iota(jnp.int32, (TARGETS, extra.shape[1]), 0)
    hit = target == extra[1:2].astype(jnp.int32)
    return jnp.where(hit, extra[0:1], 0.0).astype(BF16)


def add_piece(scores, top, piece_ref, num, den):
    expo = jnp.exp2(scores - top).astype(BF16)
    rounded = expo.astype(F32)
    for k in range(expo.shape[1] // 128):
        den = den + rounded[:, k * 128 : (k + 1) * 128]
    num = num + lax.dot_general(
        expo,
        piece_values(piece_ref),
        (((1,), (1,)), ((), ())),
        preferred_element_type=F32,
    )
    return num, den


def squared_norm(queries):
    wide = queries.astype(F32)
    return jnp.sum(wide * wide, axis=1, keepdims=True)


def first_kernel(queries_ref, piece_ref, num_ref, den_ref, top_ref):
    queries = queries_ref[...]
    rows = queries.shape[0]
    scores = piece_scores(queries, squared_norm(queries), piece_ref)
    top = jnp.max(scores, axis=1, keepdims=True) + MARGIN
    num = jnp.zeros((rows, TARGETS), F32)
    den = jnp.zeros((rows, 128), F32)
    num, den = add_piece(scores, top, piece_ref, num, den)
    num_ref[...] = num
    den_ref[...] = den
    top_ref[...] = jnp.broadcast_to(top, (rows, 128))


def more_kernel(count, *refs):
    queries_ref, num_in, den_in, top_ref = refs[:4]
    pieces = refs[4 : 4 + count]
    num_ref, den_ref = refs[4 + count :]
    queries = queries_ref[...]
    query_norm = squared_norm(queries)
    top = top_ref[:, 0:1]
    num, den = num_in[...], den_in[...]
    for piece_ref in pieces:
        scores = piece_scores(queries, query_norm, piece_ref)
        num, den = add_piece(scores, top, piece_ref, num, den)
    num_ref[...] = num
    den_ref[...] = den


def last_kernel(count, past, *refs):
    queries_ref, num_in, den_in, top_ref, weight_ref = refs[:5]
    pieces = refs[5 : 5 + count]
    earlier = refs[5 + count : 5 + count + past]
    profile_ref, moments_ref = refs[5 + count + past : 7 + count + past]
    buffers = refs[7 + count + past : -1]
    done = refs[-1]
    rows = queries_ref.shape[0]
    queries = queries_ref[...]
    query_norm = squared_norm(queries)
    top = top_ref[:, 0:1]
    num, den = num_in[...], den_in[...]
    for piece_ref in pieces:
        scores = piece_scores(queries, query_norm, piece_ref)
        num, den = add_piece(scores, top, piece_ref, num, den)
    total = jnp.sum(den, axis=1, keepdims=True)
    profile_ref[...] = num * (1.0 / total)

    @pl.when(jnp.logical_not(jnp.max(total) <= 1.0))
    def _():
        copies = [
            pltpu.make_async_copy(source, buffer, done.at[k])
            for k, (source, buffer) in enumerate(zip(earlier, buffers))
        ]
        for copy in copies:
            copy.start()
        for copy in copies:
            copy.wait()
        everything = list(pieces) + list(buffers)
        best = jnp.full((rows, 1), -1.0, F32)
        for piece_ref in everything:
            scores = piece_scores(queries, query_norm, piece_ref)
            best = jnp.maximum(best, jnp.max(scores, axis=1, keepdims=True))
        again = jnp.zeros((rows, TARGETS), F32)
        weight = jnp.zeros((rows, 128), F32)
        for piece_ref in everything:
            scores = piece_scores(queries, query_norm, piece_ref)
            again, weight = add_piece(scores, best, piece_ref, again, weight)
        profile_ref[...] = again * (1.0 / jnp.sum(weight, axis=1, keepdims=True))

    profile = profile_ref[...]
    weight = weight_ref[...]
    weight_total = jnp.sum(weight, axis=0, keepdims=True)
    first = jnp.sum(profile * weight, axis=0, keepdims=True)
    mean = first / weight_total
    spread = (profile - mean) * jnp.sqrt(weight)
    outer = (((0,), (0,)), ((), ()))
    moments = lax.dot_general(
        spread, spread, outer, precision=EXACT, preferred_element_type=F32
    ) + lax.dot_general(mean, first, outer, precision=EXACT, preferred_element_type=F32)
    row = lax.broadcasted_iota(jnp.int32, (TARGETS, TARGETS), 0)
    column = lax.broadcasted_iota(jnp.int32, (TARGETS, TARGETS), 1)
    moments = jnp.where((row == 0) & (column > 0), first, moments)
    moments = jnp.where((row == 1) & (column == 2), first[0:1, 0:1], moments)
    moments = jnp.where((row == 1) & (column == 3), weight_total, moments)
    moments_ref[...] = moments


def work(rows, pieces):
    refs = sum(piece.shape[1] for piece in pieces)
    return cost(6 * rows * refs * (BITS + TARGETS), rows * 2048 + refs * DEPTH * 2)


def first_part(queries, piece):
    rows = queries.shape[0]
    return pl.pallas_call(
        first_kernel,
        in_specs=[VMEM, VMEM],
        out_specs=[VMEM] * 3,
        out_shape=[
            jax.ShapeDtypeStruct((rows, TARGETS), F32),
            jax.ShapeDtypeStruct((rows, 128), F32),
            jax.ShapeDtypeStruct((rows, 128), F32),
        ],
        compiler_params=params(),
        cost_estimate=work(rows, [piece]),
        name="first_part",
    )(queries, piece)


def more_part(queries, state, pieces):
    rows = queries.shape[0]
    num, den = pl.pallas_call(
        functools.partial(more_kernel, len(pieces)),
        in_specs=[VMEM] * (4 + len(pieces)),
        out_specs=[VMEM] * 2,
        out_shape=[
            jax.ShapeDtypeStruct((rows, TARGETS), F32),
            jax.ShapeDtypeStruct((rows, 128), F32),
        ],
        compiler_params=params(),
        cost_estimate=work(rows, pieces),
        name="more_part",
    )(queries, *state, *pieces)
    return num, den, state[2]


def last_part(queries, state, weight, pieces, earlier):
    rows = queries.shape[0]
    return pl.pallas_call(
        functools.partial(last_kernel, len(pieces), len(earlier)),
        in_specs=[VMEM] * (5 + len(pieces)) + [pl.BlockSpec(memory_space=pl.ANY)] * len(earlier),
        out_specs=[VMEM] * 2,
        out_shape=[
            jax.ShapeDtypeStruct((rows, TARGETS), F32),
            jax.ShapeDtypeStruct((TARGETS, TARGETS), F32),
        ],
        scratch_shapes=[pltpu.VMEM(piece.shape, BF16) for piece in earlier]
        + [pltpu.SemaphoreType.DMA((len(earlier),))],
        compiler_params=params(),
        cost_estimate=work(rows, pieces),
        name="last_part",
    )(queries, *state, weight, *pieces, *earlier)


def repeat_row(block, at):
    return jnp.broadcast_to(block[at : at + 1, :], block.shape)


def inverse_factor(schur, size):
    groups = PANEL // 8
    panels = size // PANEL
    sub = lax.broadcasted_iota(jnp.int32, (8, 128), 0)
    eye = (
        lax.broadcasted_iota(jnp.int32, (PANEL, PANEL), 0)
        == lax.broadcasted_iota(jnp.int32, (PANEL, PANEL), 1)
    ).astype(F32)
    schur = [schur[i * PANEL : (i + 1) * PANEL, :] for i in range(panels)]
    inverse = [None] * panels
    result = []
    for t in range(panels):
        start = t * PANEL
        lane0 = start // 128 * 128
        left = schur[t][:, lane0:]
        right = [inverse[t]] if t else []
        right.append(eye)
        width = start + PANEL
        if width % 128:
            right.append(jnp.zeros((PANEL, -width % 128), F32))
        right = jnp.concatenate(right, axis=1)
        nl, nr = left.shape[1] // 128, right.shape[1] // 128
        tiles = [
            [left[8 * g : 8 * g + 8, 128 * k : 128 * k + 128] for k in range(nl)]
            + [right[8 * g : 8 * g + 8, 128 * k : 128 * k + 128] for k in range(nr)]
            for g in range(groups)
        ]
        square = left[:, start - lane0 : start - lane0 + PANEL]
        spread = [
            [
                jnp.broadcast_to(square[8 * g : 8 * g + 8, k : k + 1], (8, 128))
                if g >= k // 8
                else None
                for g in range(groups)
            ]
            for k in range(PANEL)
        ]
        inverses = []
        for k in range(PANEL):
            own, at = divmod(k, 8)
            inv = 1.0 / repeat_row(spread[k][own], at)
            inverses.append(inv)
            column = [
                spread[k][g] if g > own else jnp.where(sub > at, spread[k][g], 0.0) if g == own else None
                for g in range(groups)
            ]
            for m in range(k + 1, PANEL):
                factor = repeat_row(spread[k][m // 8], m % 8)
                for g in range(m // 8, groups):
                    spread[m][g] = spread[m][g] - (column[g] * factor) * inv
            multiple = [None if c is None else c * inv for c in column]
            for k2 in range(nl + nr):
                row = repeat_row(tiles[own][k2], at)
                for g in range(own, groups):
                    tiles[g][k2] = tiles[g][k2] - multiple[g] * row
        scale = []
        for g in range(groups):
            column = inverses[8 * g]
            for o in range(1, 8):
                column = jnp.where(sub == o, inverses[8 * g + o], column)
            scale.append(column)
        root = [jnp.sqrt(column) for column in scale]
        blank = [jnp.zeros((8, 128), F32)] * (size // 128 - nr)
        result.append(
            jnp.concatenate(
                [
                    jnp.concatenate([tiles[g][nl + k] * root[g] for k in range(nr)] + blank, axis=1)
                    for g in range(groups)
                ],
                axis=0,
            )
        )
        if t == panels - 1:
            break
        upper = jnp.concatenate([jnp.concatenate(tiles[g], axis=1) for g in range(groups)], axis=0)
        scaled = jnp.concatenate(
            [
                jnp.concatenate([tiles[g][k] * scale[g] for k in range(nl)], axis=1)
                for g in range(groups)
            ],
            axis=0,
        )
        for low, high in ((t + 1, t + 2), (t + 2, panels)):
            if low >= high:
                continue
            update = lax.dot_general(
                scaled[:, low * PANEL - lane0 : high * PANEL - lane0],
                upper,
                (((0,), (0,)), ((), ())),
                precision=EXACT,
                preferred_element_type=F32,
            )
            for i in range(low, high):
                part = update[(i - low) * PANEL : (i - low + 1) * PANEL]
                kept = [schur[i][:, :lane0]] if lane0 else []
                schur[i] = jnp.concatenate(kept + [schur[i][:, lane0:] - part[:, : nl * 128]], axis=1)
                fresh = -part[:, nl * 128 : nl * 128 + width]
                if inverse[i] is not None:
                    fresh = jnp.concatenate([inverse[i] + fresh[:, :start], fresh[:, start:]], axis=1)
                inverse[i] = fresh
    return jnp.concatenate(result, axis=0)


def whiten_kernel(moments_ref, profile_ref, weight_ref, out_ref):
    total = moments_ref[...]
    row = lax.broadcasted_iota(jnp.int32, (TARGETS, TARGETS), 0)
    column = lax.broadcasted_iota(jnp.int32, (TARGETS, TARGETS), 1)
    share = 1.0 / total[1:2, 3:4]
    first = jnp.where(column[0:1] == 0, total[1:2, 2:3], total[0:1, :])
    mean = first * share
    outer = lax.dot_general(
        mean, mean, (((0,), (0,)), ((), ())), precision=EXACT, preferred_element_type=F32
    )
    lower = jnp.where(column <= row, total, 0.0)
    strict = jnp.where(column < row, total, 0.0)
    covariance = (lower + strict.T) * share - outer
    covariance = covariance + jnp.where(row == column, SHRINKAGE, 0.0)
    inverse = inverse_factor(covariance, TARGETS)
    centered = (profile_ref[...] - mean) * jnp.sqrt(weight_ref[...])
    out_ref[...] = lax.dot_general(
        centered, inverse, (((1,), (1,)), ((), ())), precision=EXACT, preferred_element_type=F32
    )


def whiten(moments, profile, weight):
    return pl.pallas_call(
        whiten_kernel,
        in_specs=[VMEM, VMEM, VMEM],
        out_specs=VMEM,
        out_shape=jax.ShapeDtypeStruct(profile.shape, F32),
        compiler_params=params(),
        name="whiten",
    )(moments, profile, weight)


def on_device(compounds, compound_weight, reference_prints, potency, target_label):
    devices = lax.axis_size(ALL)
    core = lax.rem(lax.axis_index("lib"), 2).astype(jnp.int32).reshape(1)
    weight = compound_weight[:, None]
    own, half = prepare(core, reference_prints, potency[None, :], target_label[None, :])

    hold = lax.optimization_barrier
    far, flipped = send(half, up2), send(half, flip)
    above, below = send(half, up), send(half, down)
    state = first_part(compounds, own)
    flipped, above, below, state = hold((flipped, above, below, state))
    flipped_above, flipped_below = send(flipped, up), send(flipped, down)
    others = [send(piece, sibling) for piece in (flipped, above, below)]
    state = more_part(compounds, state, [flipped, above, below])
    far, others, state = hold((far, others, state))
    flipped_far, other_far = send(far, flip), send(far, sibling)
    state = more_part(compounds, state, others + [far])
    flipped_above, flipped_below, other_far, state = hold(
        (flipped_above, flipped_below, other_far, state)
    )
    other_above, other_below = send(flipped_above, sibling), send(flipped_below, sibling)
    state = more_part(compounds, state, [other_far, flipped_above, flipped_below])
    other_flipped_far = send(flipped_far, sibling)
    later = [other_above, other_below, flipped_far, other_flipped_far]
    earlier = [own, flipped, above, below, *others, far, other_far, flipped_above, flipped_below]
    profile, moments = last_part(compounds, state, weight, later, earlier)

    shares = lax.all_to_all(moments.reshape(devices, 2, TARGETS // 2), ALL, 0, 0)
    share = jnp.sum(shares, axis=0, keepdims=True)
    total = lax.all_to_all(jnp.broadcast_to(share, shares.shape), ALL, 0, 0)
    return whiten(total.reshape(TARGETS, TARGETS), profile, weight)


def solution(mesh):
    placed = (P(("lib", "ref"), None), P(("lib", "ref")), P("ref", None), P("ref"), P("ref"))
    return jax.shard_map(
        on_device, mesh=mesh, in_specs=placed, out_specs=P(("lib", "ref"), None), check_vma=False
    )
```

```python
import functools

import jax
import jax.numpy as jnp
from jax import lax
from jax.experimental import pallas as pl
from jax.experimental.pallas import tpu as pltpu
from jax.sharding import PartitionSpec as P

ALL = ("lib", "ref")
BITS = 512
EXTRA = 16
DEPTH = BITS + EXTRA
TARGETS = 256
SHRINKAGE = 0.02
LOG2E = 1.4426950408889634
SCALE = 320.0 * LOG2E
MARGIN = 58.0
PANEL = 32
REDO = 128
F32 = jnp.float32
BF16 = jnp.bfloat16
EXACT = lax.Precision.HIGHEST
VMEM = pl.BlockSpec(memory_space=pltpu.VMEM)


def params(mib=40):
    return pltpu.CompilerParams(vmem_limit_bytes=mib * 2**20)


def cost(flops, size):
    return pl.CostEstimate(flops=flops, bytes_accessed=size, transcendentals=0)


def place(x, y, z, c):
    return ((z % 8 * 2 + x % 2) * 2 + c % 2) * 8 + y % 4 * 2 + x // 2


def route(move):
    pairs = []
    for x in range(4):
        for y in range(4):
            for z in range(8):
                for c in range(2):
                    pairs.append((place(x, y, z, c), place(*move(x, y, z, c))))
    return sorted(pairs)


def send(value, move):
    return lax.ppermute(value, ALL, route(move))


def up(x, y, z, c):
    return x, y + 1, z, c


def down(x, y, z, c):
    return x, y - 1, z, c


def up2(x, y, z, c):
    return x, y + 2, z, c


def flip(x, y, z, c):
    return 3 - x, y, z, c


def sibling(x, y, z, c):
    return x, y, z, 1 - c


def prep_kernel(core_ref, prints_ref, potency_ref, label_ref, whole_ref, half_ref):
    prints = prints_ref[...].T
    wide = prints.astype(F32)
    norm = jnp.sum(wide * wide, axis=0, keepdims=True)
    high = norm.astype(BF16)
    rest = norm - high.astype(F32)
    middle = rest.astype(BF16)
    low = (rest - middle.astype(F32)).astype(BF16)
    row = lax.broadcasted_iota(jnp.int32, (EXTRA, prints.shape[1]), 0)
    extra = jnp.where(row == 0, potency_ref[...].astype(F32), 0.0)
    extra = jnp.where(row == 1, label_ref[...].astype(F32), extra)
    for at, part in ((2, high), (3, middle), (4, low)):
        extra = jnp.where(row == at, part.astype(F32), extra)
    extra = extra.astype(BF16)
    whole_ref[:BITS, :] = prints
    whole_ref[BITS:, :] = extra
    first = core_ref[0] == 0
    half = prints.shape[1] // 2

    @pl.when(first)
    def _():
        half_ref[:BITS, :] = prints[:, :half]
        half_ref[BITS:, :] = extra[:, :half]

    @pl.when(jnp.logical_not(first))
    def _():
        half_ref[:BITS, :] = prints[:, half:]
        half_ref[BITS:, :] = extra[:, half:]


def prepare(core, prints, potency, label):
    refs = prints.shape[0]
    return pl.pallas_call(
        prep_kernel,
        in_specs=[pl.BlockSpec(memory_space=pltpu.SMEM), VMEM, VMEM, VMEM],
        out_specs=[VMEM, VMEM],
        out_shape=[
            jax.ShapeDtypeStruct((DEPTH, refs), BF16),
            jax.ShapeDtypeStruct((DEPTH, refs // 2), BF16),
        ],
        compiler_params=params(),
        name="prepare",
    )(core, prints, potency, label)


def piece_scores(queries, query_norm, piece_ref):
    extra = piece_ref[BITS:, :].astype(F32)
    norm = extra[2:3] + extra[3:4] + extra[4:5]
    inter = jnp.dot(queries, piece_ref[:BITS, :], preferred_element_type=F32)
    inverse = 1.0 / ((query_norm + norm) - inter)
    return (inter * inverse) * SCALE


def piece_values(piece_ref):
    extra = piece_ref[BITS:, :].astype(F32)
    target = lax.broadcasted_iota(jnp.int32, (TARGETS, extra.shape[1]), 0)
    hit = target == extra[1:2].astype(jnp.int32)
    return jnp.where(hit, extra[0:1], 0.0).astype(BF16)


def add_piece(scores, top, piece_ref, num, den):
    expo = jnp.exp2(scores - top).astype(BF16)
    rounded = expo.astype(F32)
    for k in range(expo.shape[1] // 128):
        den = den + rounded[:, k * 128 : (k + 1) * 128]
    num = num + lax.dot_general(
        expo,
        piece_values(piece_ref),
        (((1,), (1,)), ((), ())),
        preferred_element_type=F32,
    )
    return num, den


def squared_norm(queries):
    wide = queries.astype(F32)
    return jnp.sum(wide * wide, axis=1, keepdims=True)


def first_kernel(queries_ref, piece_ref, num_ref, den_ref, top_ref):
    queries = queries_ref[...]
    rows = queries.shape[0]
    scores = piece_scores(queries, squared_norm(queries), piece_ref)
    top = jnp.max(scores, axis=1, keepdims=True) + MARGIN
    num = jnp.zeros((rows, TARGETS), F32)
    den = jnp.zeros((rows, 128), F32)
    num, den = add_piece(scores, top, piece_ref, num, den)
    num_ref[...] = num
    den_ref[...] = den
    top_ref[...] = jnp.broadcast_to(top, (rows, 128))


def more_kernel(count, *refs):
    queries_ref, num_in, den_in, top_ref = refs[:4]
    pieces = refs[4 : 4 + count]
    num_ref, den_ref = refs[4 + count :]
    queries = queries_ref[...]
    query_norm = squared_norm(queries)
    top = top_ref[:, 0:1]
    num, den = num_in[...], den_in[...]
    for piece_ref in pieces:
        scores = piece_scores(queries, query_norm, piece_ref)
        num, den = add_piece(scores, top, piece_ref, num, den)
    num_ref[...] = num
    den_ref[...] = den


def last_kernel(count, past, *refs):
    queries_ref, num_in, den_in, top_ref, weight_ref = refs[:5]
    pieces = refs[5 : 5 + count]
    earlier = refs[5 + count : 5 + count + past]
    profile_ref, moments_ref = refs[5 + count + past : 7 + count + past]
    buffer, done = refs[7 + count + past :]
    rows = queries_ref.shape[0]
    queries = queries_ref[...]
    query_norm = squared_norm(queries)
    top = top_ref[:, 0:1]
    num, den = num_in[...], den_in[...]
    for piece_ref in pieces:
        scores = piece_scores(queries, query_norm, piece_ref)
        num, den = add_piece(scores, top, piece_ref, num, den)
    total = jnp.sum(den, axis=1, keepdims=True)
    profile_ref[...] = num * (1.0 / total)

    @pl.when(jnp.logical_not(jnp.max(total) <= 1.0))
    def _():
        width = pieces[0].shape[1]
        sources = list(pieces)
        for source in earlier:
            sources += [source.at[:, pl.ds(k, width)] for k in range(0, source.shape[1], width)]
        copies = [
            pltpu.make_async_copy(source, buffer.at[k], done.at[k])
            for k, source in enumerate(sources)
        ]
        for copy in copies:
            copy.start()
        for copy in copies:
            copy.wait()

        @pl.loop(0, rows // REDO)
        def _(block):
            here = pl.ds(pl.multiple_of(block * REDO, REDO), REDO)
            queries = queries_ref[here, :]
            query_norm = squared_norm(queries)

            def highest(k, best):
                scores = piece_scores(queries, query_norm, buffer.at[k])
                return jnp.maximum(best, jnp.max(scores, axis=1, keepdims=True))

            def collect(k, sums):
                scores = piece_scores(queries, query_norm, buffer.at[k])
                return add_piece(scores, best, buffer.at[k], *sums)

            best = lax.fori_loop(0, len(sources), highest, jnp.full((REDO, 1), -1.0, F32))
            blank = jnp.zeros((REDO, TARGETS), F32), jnp.zeros((REDO, 128), F32)
            num, den = lax.fori_loop(0, len(sources), collect, blank)
            profile_ref[here, :] = num * (1.0 / jnp.sum(den, axis=1, keepdims=True))

    profile = profile_ref[...]
    weight = weight_ref[...]
    weight_total = jnp.sum(weight, axis=0, keepdims=True)
    first = jnp.sum(profile * weight, axis=0, keepdims=True)
    mean = first / weight_total
    spread = (profile - mean) * jnp.sqrt(weight)
    outer = (((0,), (0,)), ((), ()))
    moments = lax.dot_general(
        spread, spread, outer, precision=EXACT, preferred_element_type=F32
    ) + lax.dot_general(mean, first, outer, precision=EXACT, preferred_element_type=F32)
    row = lax.broadcasted_iota(jnp.int32, (TARGETS, TARGETS), 0)
    column = lax.broadcasted_iota(jnp.int32, (TARGETS, TARGETS), 1)
    moments = jnp.where((row == 0) & (column > 0), first, moments)
    moments = jnp.where((row == 1) & (column == 2), first[0:1, 0:1], moments)
    moments = jnp.where((row == 1) & (column == 3), weight_total, moments)
    moments_ref[...] = moments


def work(rows, pieces):
    refs = sum(piece.shape[1] for piece in pieces)
    return cost(6 * rows * refs * (BITS + TARGETS), rows * 2048 + refs * DEPTH * 2)


def first_part(queries, piece):
    rows = queries.shape[0]
    return pl.pallas_call(
        first_kernel,
        in_specs=[VMEM, VMEM],
        out_specs=[VMEM] * 3,
        out_shape=[
            jax.ShapeDtypeStruct((rows, TARGETS), F32),
            jax.ShapeDtypeStruct((rows, 128), F32),
            jax.ShapeDtypeStruct((rows, 128), F32),
        ],
        compiler_params=params(),
        cost_estimate=work(rows, [piece]),
        name="first_part",
    )(queries, piece)


def more_part(queries, state, pieces):
    rows = queries.shape[0]
    num, den = pl.pallas_call(
        functools.partial(more_kernel, len(pieces)),
        in_specs=[VMEM] * (4 + len(pieces)),
        out_specs=[VMEM] * 2,
        out_shape=[
            jax.ShapeDtypeStruct((rows, TARGETS), F32),
            jax.ShapeDtypeStruct((rows, 128), F32),
        ],
        compiler_params=params(),
        cost_estimate=work(rows, pieces),
        name="more_part",
    )(queries, *state, *pieces)
    return num, den, state[2]


def last_part(queries, state, weight, pieces, earlier):
    rows, width = queries.shape[0], pieces[0].shape[1]
    count = sum(piece.shape[1] // width for piece in [*pieces, *earlier])
    return pl.pallas_call(
        functools.partial(last_kernel, len(pieces), len(earlier)),
        in_specs=[VMEM] * (5 + len(pieces)) + [pl.BlockSpec(memory_space=pl.ANY)] * len(earlier),
        out_specs=[VMEM] * 2,
        out_shape=[
            jax.ShapeDtypeStruct((rows, TARGETS), F32),
            jax.ShapeDtypeStruct((TARGETS, TARGETS), F32),
        ],
        scratch_shapes=[pltpu.VMEM((count, DEPTH, width), BF16), pltpu.SemaphoreType.DMA((count,))],
        compiler_params=params(),
        cost_estimate=work(rows, pieces),
        name="last_part",
    )(queries, *state, weight, *pieces, *earlier)


def repeat_row(block, at):
    return jnp.broadcast_to(block[at : at + 1, :], block.shape)


def inverse_factor(schur, size):
    groups = PANEL // 8
    panels = size // PANEL
    sub = lax.broadcasted_iota(jnp.int32, (8, 128), 0)
    eye = (
        lax.broadcasted_iota(jnp.int32, (PANEL, PANEL), 0)
        == lax.broadcasted_iota(jnp.int32, (PANEL, PANEL), 1)
    ).astype(F32)
    schur = [schur[i * PANEL : (i + 1) * PANEL, :] for i in range(panels)]
    inverse = [None] * panels
    result = []
    for t in range(panels):
        start = t * PANEL
        lane0 = start // 128 * 128
        left = schur[t][:, lane0:]
        right = [inverse[t]] if t else []
        right.append(eye)
        width = start + PANEL
        if width % 128:
            right.append(jnp.zeros((PANEL, -width % 128), F32))
        right = jnp.concatenate(right, axis=1)
        nl, nr = left.shape[1] // 128, right.shape[1] // 128
        tiles = [
            [left[8 * g : 8 * g + 8, 128 * k : 128 * k + 128] for k in range(nl)]
            + [right[8 * g : 8 * g + 8, 128 * k : 128 * k + 128] for k in range(nr)]
            for g in range(groups)
        ]
        square = left[:, start - lane0 : start - lane0 + PANEL]
        spread = [
            [
                jnp.broadcast_to(square[8 * g : 8 * g + 8, k : k + 1], (8, 128))
                if g >= k // 8
                else None
                for g in range(groups)
            ]
            for k in range(PANEL)
        ]
        inverses = []
        for k in range(PANEL):
            own, at = divmod(k, 8)
            inv = 1.0 / repeat_row(spread[k][own], at)
            inverses.append(inv)
            column = [
                spread[k][g] if g > own else jnp.where(sub > at, spread[k][g], 0.0) if g == own else None
                for g in range(groups)
            ]
            for m in range(k + 1, PANEL):
                factor = repeat_row(spread[k][m // 8], m % 8)
                for g in range(m // 8, groups):
                    spread[m][g] = spread[m][g] - (column[g] * factor) * inv
            multiple = [None if c is None else c * inv for c in column]
            for k2 in range(nl + nr):
                row = repeat_row(tiles[own][k2], at)
                for g in range(own, groups):
                    tiles[g][k2] = tiles[g][k2] - multiple[g] * row
        scale = []
        for g in range(groups):
            column = inverses[8 * g]
            for o in range(1, 8):
                column = jnp.where(sub == o, inverses[8 * g + o], column)
            scale.append(column)
        root = [jnp.sqrt(column) for column in scale]
        blank = [jnp.zeros((8, 128), F32)] * (size // 128 - nr)
        result.append(
            jnp.concatenate(
                [
                    jnp.concatenate([tiles[g][nl + k] * root[g] for k in range(nr)] + blank, axis=1)
                    for g in range(groups)
                ],
                axis=0,
            )
        )
        if t == panels - 1:
            break
        upper = jnp.concatenate([jnp.concatenate(tiles[g], axis=1) for g in range(groups)], axis=0)
        scaled = jnp.concatenate(
            [
                jnp.concatenate([tiles[g][k] * scale[g] for k in range(nl)], axis=1)
                for g in range(groups)
            ],
            axis=0,
        )
        for low, high in ((t + 1, t + 2), (t + 2, panels)):
            if low >= high:
                continue
            update = lax.dot_general(
                scaled[:, low * PANEL - lane0 : high * PANEL - lane0],
                upper,
                (((0,), (0,)), ((), ())),
                precision=EXACT,
                preferred_element_type=F32,
            )
            for i in range(low, high):
                part = update[(i - low) * PANEL : (i - low + 1) * PANEL]
                kept = [schur[i][:, :lane0]] if lane0 else []
                schur[i] = jnp.concatenate(kept + [schur[i][:, lane0:] - part[:, : nl * 128]], axis=1)
                fresh = -part[:, nl * 128 : nl * 128 + width]
                if inverse[i] is not None:
                    fresh = jnp.concatenate([inverse[i] + fresh[:, :start], fresh[:, start:]], axis=1)
                inverse[i] = fresh
    return jnp.concatenate(result, axis=0)


def whiten_kernel(moments_ref, profile_ref, weight_ref, out_ref):
    total = moments_ref[...]
    row = lax.broadcasted_iota(jnp.int32, (TARGETS, TARGETS), 0)
    column = lax.broadcasted_iota(jnp.int32, (TARGETS, TARGETS), 1)
    share = 1.0 / total[1:2, 3:4]
    first = jnp.where(column[0:1] == 0, total[1:2, 2:3], total[0:1, :])
    mean = first * share
    outer = lax.dot_general(
        mean, mean, (((0,), (0,)), ((), ())), precision=EXACT, preferred_element_type=F32
    )
    lower = jnp.where(column <= row, total, 0.0)
    strict = jnp.where(column < row, total, 0.0)
    covariance = (lower + strict.T) * share - outer
    covariance = covariance + jnp.where(row == column, SHRINKAGE, 0.0)
    inverse = inverse_factor(covariance, TARGETS)
    centered = (profile_ref[...] - mean) * jnp.sqrt(weight_ref[...])
    out_ref[...] = lax.dot_general(
        centered, inverse, (((1,), (1,)), ((), ())), precision=EXACT, preferred_element_type=F32
    )


def whiten(moments, profile, weight):
    return pl.pallas_call(
        whiten_kernel,
        in_specs=[VMEM, VMEM, VMEM],
        out_specs=VMEM,
        out_shape=jax.ShapeDtypeStruct(profile.shape, F32),
        compiler_params=params(),
        name="whiten",
    )(moments, profile, weight)


def on_device(compounds, compound_weight, reference_prints, potency, target_label):
    devices = lax.axis_size(ALL)
    core = lax.rem(lax.axis_index("lib"), 2).astype(jnp.int32).reshape(1)
    weight = compound_weight[:, None]
    own, half = prepare(core, reference_prints, potency[None, :], target_label[None, :])

    hold = lax.optimization_barrier
    far, flipped = send(half, up2), send(half, flip)
    above, below = send(half, up), send(half, down)
    state = first_part(compounds, own)
    flipped, above, below, state = hold((flipped, above, below, state))
    flipped_above, flipped_below = send(flipped, up), send(flipped, down)
    others = [send(piece, sibling) for piece in (flipped, above, below)]
    state = more_part(compounds, state, [flipped, above, below])
    far, others, state = hold((far, others, state))
    flipped_far, other_far = send(far, flip), send(far, sibling)
    state = more_part(compounds, state, others + [far])
    flipped_above, flipped_below, other_far, state = hold(
        (flipped_above, flipped_below, other_far, state)
    )
    other_above, other_below = send(flipped_above, sibling), send(flipped_below, sibling)
    state = more_part(compounds, state, [other_far, flipped_above, flipped_below])
    other_flipped_far = send(flipped_far, sibling)
    later = [other_above, other_below, flipped_far, other_flipped_far]
    earlier = [own, flipped, above, below, *others, far, other_far, flipped_above, flipped_below]
    profile, moments = last_part(compounds, state, weight, later, earlier)

    shares = lax.all_to_all(moments.reshape(devices, 2, TARGETS // 2), ALL, 0, 0)
    share = jnp.sum(shares, axis=0, keepdims=True)
    total = lax.all_to_all(jnp.broadcast_to(share, shares.shape), ALL, 0, 0)
    return whiten(total.reshape(TARGETS, TARGETS), profile, weight)


def solution(mesh):
    placed = (P(("lib", "ref"), None), P(("lib", "ref")), P("ref", None), P("ref"), P("ref"))
    return jax.shard_map(
        on_device, mesh=mesh, in_specs=placed, out_specs=P(("lib", "ref"), None), check_vma=False
    )
```

```python
import functools

import jax
import jax.numpy as jnp
from jax import lax
from jax.experimental import pallas as pl
from jax.experimental.pallas import tpu as pltpu
from jax.sharding import PartitionSpec as P

ALL = ("z", "x_lo", "core", "y", "x_hi")
PLANE = ("x_lo", "core", "y", "x_hi")
BITS = 512
EXTRA = 16
DEPTH = BITS + EXTRA
TARGETS = 256
SHRINKAGE = 0.02
LOG2E = 1.4426950408889634
SCALE = 320.0 * LOG2E
MARGIN = 58.0
PANEL = 32
REDO = 128
F32 = jnp.float32
BF16 = jnp.bfloat16
EXACT = lax.Precision.HIGHEST
VMEM = pl.BlockSpec(memory_space=pltpu.VMEM)


def params(mib=20):
    return pltpu.CompilerParams(vmem_limit_bytes=mib * 2**20)


def cost(flops, size):
    return pl.CostEstimate(flops=flops, bytes_accessed=size, transcendentals=0)


def place(x, y, z, c):
    return ((z % 8 * 2 + x % 2) * 2 + c % 2) * 8 + y % 4 * 2 + x // 2


def route(move):
    pairs = []
    for x in range(4):
        for y in range(4):
            for z in range(8):
                for c in range(2):
                    pairs.append((place(x, y, z, c), place(*move(x, y, z, c))))
    return sorted(pairs)


def send(value, move):
    return lax.ppermute(value, ALL, route(move))


def up(x, y, z, c):
    return x, y + 1, z, c


def down(x, y, z, c):
    return x, y - 1, z, c


def flip(x, y, z, c):
    return 3 - x, y, z, c


def onward(x, y, z, c):
    return x, y + 1 - 2 * c, z, c


def across(x, y, z, c):
    return 3 - x, y + 1 - 2 * c, z, c


def sibling(x, y, z, c):
    return x, y, z, 1 - c


def prep_kernel(core_ref, prints_ref, marks_ref, whole_ref, half_ref):
    prints = prints_ref[...].T
    wide = prints.astype(F32)
    norm = jnp.sum(wide * wide, axis=0, keepdims=True)
    high = norm.astype(BF16)
    rest = norm - high.astype(F32)
    middle = rest.astype(BF16)
    low = (rest - middle.astype(F32)).astype(BF16)
    row = lax.broadcasted_iota(jnp.int32, (EXTRA, prints.shape[1]), 0)
    extra = jnp.where(row == 0, marks_ref[0:1, :], 0.0)
    extra = jnp.where(row == 1, marks_ref[1:2, :], extra)
    for at, part in ((2, high), (3, middle), (4, low)):
        extra = jnp.where(row == at, part.astype(F32), extra)
    extra = extra.astype(BF16)
    half = prints.shape[1] // 2

    def store(mine, other):
        for ref in (whole_ref, half_ref):
            ref[:BITS, :half] = prints[:, mine]
            ref[BITS:, :half] = extra[:, mine]
        whole_ref[:BITS, half:] = prints[:, other]
        whole_ref[BITS:, half:] = extra[:, other]

    @pl.when(core_ref[0] == 0)
    def _():
        store(slice(0, half), slice(half, None))

    @pl.when(core_ref[0] != 0)
    def _():
        store(slice(half, None), slice(0, half))


def prepare(core, prints, marks):
    refs = prints.shape[0]
    return pl.pallas_call(
        prep_kernel,
        in_specs=[pl.BlockSpec(memory_space=pltpu.SMEM), VMEM, VMEM],
        out_specs=[VMEM, VMEM],
        out_shape=[
            jax.ShapeDtypeStruct((DEPTH, refs), BF16),
            jax.ShapeDtypeStruct((DEPTH, refs // 2), BF16),
        ],
        compiler_params=params(),
        name="prepare",
    )(core, prints, marks)


def piece_scores(queries, query_norm, piece_ref):
    extra = piece_ref[BITS:, :].astype(F32)
    norm = extra[2:3] + extra[3:4] + extra[4:5]
    inter = jnp.dot(queries, piece_ref[:BITS, :], preferred_element_type=F32)
    inverse = 1.0 / ((query_norm + norm) - inter)
    return (inter * inverse) * SCALE


def piece_values(piece_ref):
    extra = piece_ref[BITS:, :].astype(F32)
    target = lax.broadcasted_iota(jnp.int32, (TARGETS, extra.shape[1]), 0)
    hit = target == extra[1:2].astype(jnp.int32)
    return jnp.where(hit, extra[0:1], 0.0).astype(BF16)


def add_piece(scores, top, piece_ref, num, den):
    expo = jnp.exp2(scores - top).astype(BF16)
    rounded = expo.astype(F32)
    for k in range(expo.shape[1] // 128):
        den = den + rounded[:, k * 128 : (k + 1) * 128]
    num = num + lax.dot_general(
        expo,
        piece_values(piece_ref),
        (((1,), (1,)), ((), ())),
        preferred_element_type=F32,
    )
    return num, den


def squared_norm(queries):
    wide = queries.astype(F32)
    return jnp.sum(wide * wide, axis=1, keepdims=True)


def unpack(state):
    num, marks = state[:, :TARGETS], state[:, TARGETS:]
    lane = lax.broadcasted_iota(jnp.int32, marks.shape, 1)
    return num, jnp.where(lane == 1, marks, 0.0), marks[:, 0:1]


def pack(num, den, top):
    lane = lax.broadcasted_iota(jnp.int32, den.shape, 1)
    marks = jnp.where(lane == 0, top, jnp.sum(den, axis=1, keepdims=True))
    return jnp.concatenate([num, marks], axis=1)


def empty(rows):
    return jnp.zeros((rows, TARGETS), F32), jnp.zeros((rows, 128), F32)


def add_pieces(queries_ref, state_in, state_ref, pieces):
    queries = queries_ref[...]
    query_norm = squared_norm(queries)
    if state_in is None:
        num, den = empty(queries.shape[0])
        top = None
    else:
        num, den, top = unpack(state_in[...])
    for piece_ref in pieces:
        scores = piece_scores(queries, query_norm, piece_ref)
        if top is None:
            top = jnp.max(scores, axis=1, keepdims=True) + MARGIN
        num, den = add_piece(scores, top, piece_ref, num, den)
    fits = jnp.max(den) <= 1.0

    @pl.when(fits)
    def _():
        state_ref[...] = pack(num, den, top)

    @pl.when(jnp.logical_not(fits))
    def _():
        @pl.loop(0, queries_ref.shape[0] // REDO)
        def _(block):
            here = pl.ds(pl.multiple_of(block * REDO, REDO), REDO)
            queries = queries_ref[here, :]
            query_norm = squared_norm(queries)
            best = jnp.zeros((REDO, 1), F32)
            for piece_ref in pieces:
                scores = piece_scores(queries, query_norm, piece_ref)
                best = jnp.maximum(best, jnp.max(scores, axis=1, keepdims=True))
            if state_in is None:
                top = best + MARGIN
                num, den = empty(REDO)
            else:
                num, den, old = unpack(state_in[here, :])
                top = jnp.maximum(old, best + MARGIN)
                scale = jnp.exp2(old - top)
                num, den = num * scale, den * scale
            for piece_ref in pieces:
                scores = piece_scores(queries, query_norm, piece_ref)
                num, den = add_piece(scores, top, piece_ref, num, den)
            state_ref[here, :] = pack(num, den, top)


def first_kernel(queries_ref, *refs):
    add_pieces(queries_ref, None, refs[-1], refs[:-1])


def more_kernel(queries_ref, state_in, *refs):
    add_pieces(queries_ref, state_in, refs[-1], refs[:-1])


def last_kernel(count, queries_ref, state_in, weight_ref, *refs):
    state_ref, profile_ref, moments_ref = refs[count:]
    add_pieces(queries_ref, state_in, state_ref, refs[:count])
    num, den, _ = unpack(state_ref[...])
    profile = num * (1.0 / jnp.sum(den, axis=1, keepdims=True))
    profile_ref[...] = profile
    weight = weight_ref[...]
    weight_total = jnp.sum(weight, axis=0, keepdims=True)
    first = jnp.sum(profile * weight, axis=0, keepdims=True)
    mean = first / weight_total
    spread = (profile - mean) * jnp.sqrt(weight)
    outer = (((0,), (0,)), ((), ()))
    moments = lax.dot_general(
        spread, spread, outer, precision=EXACT, preferred_element_type=F32
    ) + lax.dot_general(mean, first, outer, precision=EXACT, preferred_element_type=F32)
    row = lax.broadcasted_iota(jnp.int32, (TARGETS, TARGETS), 0)
    column = lax.broadcasted_iota(jnp.int32, (TARGETS, TARGETS), 1)
    moments = jnp.where((row == 0) & (column > 0), first, moments)
    moments = jnp.where((row == 1) & (column == 2), first[0:1, 0:1], moments)
    moments = jnp.where((row == 1) & (column == 3), weight_total, moments)
    moments_ref[...] = moments


def work(rows, pieces):
    refs = sum(piece.shape[1] for piece in pieces)
    return cost(6 * rows * refs * (BITS + TARGETS), rows * 2048 + refs * DEPTH * 2)


def state_shape(rows):
    return jax.ShapeDtypeStruct((rows, TARGETS + 128), F32)


def first_part(queries, pieces):
    rows = queries.shape[0]
    return pl.pallas_call(
        first_kernel,
        in_specs=[VMEM] * (1 + len(pieces)),
        out_specs=VMEM,
        out_shape=state_shape(rows),
        compiler_params=params(),
        cost_estimate=work(rows, pieces),
        name="first_part",
    )(queries, *pieces)


def more_part(queries, state, pieces):
    rows = queries.shape[0]
    return pl.pallas_call(
        more_kernel,
        in_specs=[VMEM] * (2 + len(pieces)),
        out_specs=VMEM,
        out_shape=state_shape(rows),
        input_output_aliases={1: 0},
        compiler_params=params(),
        cost_estimate=work(rows, pieces),
        name="more_part",
    )(queries, state, *pieces)


def last_part(queries, state, weight, pieces):
    rows = queries.shape[0]
    _, profile, moments = pl.pallas_call(
        functools.partial(last_kernel, len(pieces)),
        in_specs=[VMEM] * (3 + len(pieces)),
        out_specs=[VMEM] * 3,
        out_shape=[
            state_shape(rows),
            jax.ShapeDtypeStruct((rows, TARGETS), F32),
            jax.ShapeDtypeStruct((TARGETS, TARGETS), F32),
        ],
        input_output_aliases={1: 0},
        compiler_params=params(),
        cost_estimate=work(rows, pieces),
        name="last_part",
    )(queries, state, weight, *pieces)
    return profile, moments


def repeat_row(block, at):
    return jnp.broadcast_to(block[at : at + 1, :], block.shape)


def inverse_factor(schur, size):
    groups = PANEL // 8
    panels = size // PANEL
    sub = lax.broadcasted_iota(jnp.int32, (8, 128), 0)
    eye = (
        lax.broadcasted_iota(jnp.int32, (PANEL, PANEL), 0)
        == lax.broadcasted_iota(jnp.int32, (PANEL, PANEL), 1)
    ).astype(F32)
    schur = [schur[i * PANEL : (i + 1) * PANEL, :] for i in range(panels)]
    inverse = [None] * panels
    result = []
    for t in range(panels):
        start = t * PANEL
        lane0 = start // 128 * 128
        left = schur[t][:, lane0:]
        right = [inverse[t]] if t else []
        right.append(eye)
        width = start + PANEL
        if width % 128:
            right.append(jnp.zeros((PANEL, -width % 128), F32))
        right = jnp.concatenate(right, axis=1)
        nl, nr = left.shape[1] // 128, right.shape[1] // 128
        tiles = [
            [left[8 * g : 8 * g + 8, 128 * k : 128 * k + 128] for k in range(nl)]
            + [right[8 * g : 8 * g + 8, 128 * k : 128 * k + 128] for k in range(nr)]
            for g in range(groups)
        ]
        square = left[:, start - lane0 : start - lane0 + PANEL]
        spread = [
            [
                jnp.broadcast_to(square[8 * g : 8 * g + 8, k : k + 1], (8, 128))
                if g >= k // 8
                else None
                for g in range(groups)
            ]
            for k in range(PANEL)
        ]
        inverses = []
        for k in range(PANEL):
            own, at = divmod(k, 8)
            inv = 1.0 / repeat_row(spread[k][own], at)
            inverses.append(inv)
            column = [
                spread[k][g] if g > own else jnp.where(sub > at, spread[k][g], 0.0) if g == own else None
                for g in range(groups)
            ]
            for m in range(k + 1, PANEL):
                factor = repeat_row(spread[k][m // 8], m % 8)
                for g in range(m // 8, groups):
                    spread[m][g] = spread[m][g] - (column[g] * factor) * inv
            multiple = [None if c is None else c * inv for c in column]
            for k2 in range(nl + nr):
                row = repeat_row(tiles[own][k2], at)
                for g in range(own, groups):
                    tiles[g][k2] = tiles[g][k2] - multiple[g] * row
        scale = []
        for g in range(groups):
            column = inverses[8 * g]
            for o in range(1, 8):
                column = jnp.where(sub == o, inverses[8 * g + o], column)
            scale.append(column)
        root = [jnp.sqrt(column) for column in scale]
        blank = [jnp.zeros((8, 128), F32)] * (size // 128 - nr)
        result.append(
            jnp.concatenate(
                [
                    jnp.concatenate([tiles[g][nl + k] * root[g] for k in range(nr)] + blank, axis=1)
                    for g in range(groups)
                ],
                axis=0,
            )
        )
        if t == panels - 1:
            break
        upper = jnp.concatenate([jnp.concatenate(tiles[g], axis=1) for g in range(groups)], axis=0)
        scaled = jnp.concatenate(
            [
                jnp.concatenate([tiles[g][k] * scale[g] for k in range(nl)], axis=1)
                for g in range(groups)
            ],
            axis=0,
        )
        for low, high in ((t + 1, t + 2), (t + 2, panels)):
            if low >= high:
                continue
            update = lax.dot_general(
                scaled[:, low * PANEL - lane0 : high * PANEL - lane0],
                upper,
                (((0,), (0,)), ((), ())),
                precision=EXACT,
                preferred_element_type=F32,
            )
            for i in range(low, high):
                part = update[(i - low) * PANEL : (i - low + 1) * PANEL]
                kept = [schur[i][:, :lane0]] if lane0 else []
                schur[i] = jnp.concatenate(kept + [schur[i][:, lane0:] - part[:, : nl * 128]], axis=1)
                fresh = -part[:, nl * 128 : nl * 128 + width]
                if inverse[i] is not None:
                    fresh = jnp.concatenate([inverse[i] + fresh[:, :start], fresh[:, start:]], axis=1)
                inverse[i] = fresh
    return jnp.concatenate(result, axis=0)


def whiten_kernel(moments_ref, profile_ref, weight_ref, out_ref):
    total = moments_ref[...]
    row = lax.broadcasted_iota(jnp.int32, (TARGETS, TARGETS), 0)
    column = lax.broadcasted_iota(jnp.int32, (TARGETS, TARGETS), 1)
    share = 1.0 / total[1:2, 3:4]
    first = jnp.where(column[0:1] == 0, total[1:2, 2:3], total[0:1, :])
    mean = first * share
    outer = lax.dot_general(
        mean, mean, (((0,), (0,)), ((), ())), precision=EXACT, preferred_element_type=F32
    )
    lower = jnp.where(column <= row, total, 0.0)
    strict = jnp.where(column < row, total, 0.0)
    covariance = (lower + strict.T) * share - outer
    covariance = covariance + jnp.where(row == column, SHRINKAGE, 0.0)
    inverse = inverse_factor(covariance, TARGETS)
    centered = (profile_ref[...] - mean) * jnp.sqrt(weight_ref[...])
    out_ref[...] = lax.dot_general(
        centered, inverse, (((1,), (1,)), ((), ())), precision=EXACT, preferred_element_type=F32
    )


def whiten(moments, profile, weight):
    return pl.pallas_call(
        whiten_kernel,
        in_specs=[VMEM, VMEM, VMEM],
        out_specs=VMEM,
        out_shape=jax.ShapeDtypeStruct(profile.shape, F32),
        compiler_params=params(),
        name="whiten",
    )(moments, profile, weight)


def all_sum(moments):
    plane, line = lax.axis_size(PLANE), lax.axis_size("z")
    rows = TARGETS // plane
    parts = lax.all_to_all(moments.reshape(plane, rows, TARGETS), PLANE, 0, 0)
    part = jnp.sum(parts, axis=0, keepdims=True)
    parts = lax.all_to_all(jnp.broadcast_to(part, (line, rows, TARGETS)), "z", 0, 0)
    part = jnp.sum(parts, axis=0, keepdims=True)
    parts = lax.all_to_all(jnp.broadcast_to(part, (plane, rows, TARGETS)), PLANE, 0, 0)
    return parts.reshape(TARGETS, TARGETS)


def on_device(compounds, compound_weight, reference_prints, potency, target_label):
    core = lax.axis_index("core").astype(jnp.int32).reshape(1)
    weight = compound_weight[:, None]
    marks = jnp.stack([potency.astype(F32), target_label.astype(F32)])
    own, half = prepare(core, reference_prints, marks)
    width = half.shape[1]

    hold = lax.optimization_barrier
    beside, flipped = send(own, onward), send(half, flip)
    beside, flipped = hold((beside, flipped))
    ahead, behind = send(flipped, up), send(flipped, down)
    passing = beside[:, :width]
    far, flipped_far = send(passing, onward), send(passing, across)
    near = [beside, flipped, send(beside, sibling), send(flipped, sibling)]
    state = first_part(compounds, [own] + near)
    far, flipped_far, ahead, behind, state = hold((far, flipped_far, ahead, behind, state))
    last = [far, flipped_far, ahead, behind]
    others = [send(piece, sibling) for piece in last]
    state = more_part(compounds, state, last)
    profile, moments = last_part(compounds, state, weight, others)
    return whiten(all_sum(moments), profile, weight)


def solution(mesh):
    sizes = dict(core=2, x_lo=2, x_hi=2)
    sizes["z"] = mesh.shape["lib"] // (sizes["core"] * sizes["x_lo"])
    sizes["y"] = mesh.shape["ref"] // sizes["x_hi"]
    fine = jax.sharding.Mesh(mesh.devices.reshape([sizes[name] for name in ALL]), ALL)
    spread = ALL
    across_refs = ("y", "x_hi")
    placed = (P(spread, None), P(spread), P(across_refs, None), P(across_refs), P(across_refs))
    return jax.shard_map(
        on_device, mesh=fine, in_specs=placed, out_specs=P(spread, None), check_vma=False
    )
```

```python
import functools

import jax
import jax.numpy as jnp
from jax import lax
from jax.experimental import pallas as pl
from jax.experimental.pallas import tpu as pltpu
from jax.sharding import PartitionSpec as P

ALL = ("z", "x_lo", "core", "y", "x_hi")
PLANE = ("x_lo", "core", "y", "x_hi")
BITS = 512
EXTRA = 16
DEPTH = BITS + EXTRA
TARGETS = 256
SHRINKAGE = 0.02
LOG2E = 1.4426950408889634
SCALE = 320.0 * LOG2E
MARGIN = 58.0
PANEL = 32
REDO = 128
F32 = jnp.float32
BF16 = jnp.bfloat16
EXACT = lax.Precision.HIGHEST
VMEM = pl.BlockSpec(memory_space=pltpu.VMEM)


def params(mib=20):
    return pltpu.CompilerParams(vmem_limit_bytes=mib * 2**20)


def cost(flops, size):
    return pl.CostEstimate(flops=flops, bytes_accessed=size, transcendentals=0)


def place(x, y, z, c):
    return ((z % 8 * 2 + x % 2) * 2 + c % 2) * 8 + y % 4 * 2 + x // 2


def route(move):
    pairs = []
    for x in range(4):
        for y in range(4):
            for z in range(8):
                for c in range(2):
                    pairs.append((place(x, y, z, c), place(*move(x, y, z, c))))
    return sorted(pairs)


def send(value, move):
    return lax.ppermute(value, ALL, route(move))


def flip(x, y, z, c):
    return 3 - x, y, z, c


def onward(x, y, z, c):
    return x, y + 1 - 2 * c, z, c


def across(x, y, z, c):
    return 3 - x, y + 1 - 2 * c, z, c


def sibling(x, y, z, c):
    return x, y, z, 1 - c


def prep_kernel(core_ref, prints_ref, marks_ref, mine_ref, other_ref):
    prints = prints_ref[...].T
    wide = prints.astype(F32)
    norm = jnp.sum(wide * wide, axis=0, keepdims=True)
    high = norm.astype(BF16)
    rest = norm - high.astype(F32)
    middle = rest.astype(BF16)
    low = (rest - middle.astype(F32)).astype(BF16)
    marks = marks_ref[...]
    label = jnp.floor(marks * (1.0 / 16.0))
    row = lax.broadcasted_iota(jnp.int32, (EXTRA, prints.shape[1]), 0)
    extra = jnp.where(row == 0, marks - 16.0 * label, 0.0)
    extra = jnp.where(row == 1, label, extra)
    for at, part in ((2, high), (3, middle), (4, low)):
        extra = jnp.where(row == at, part.astype(F32), extra)
    extra = extra.astype(BF16)
    half = prints.shape[1] // 2

    def store(mine, other):
        for ref, part in ((mine_ref, mine), (other_ref, other)):
            ref[:BITS, :] = prints[:, part]
            ref[BITS:, :] = extra[:, part]

    @pl.when(core_ref[0] == 0)
    def _():
        store(slice(0, half), slice(half, None))

    @pl.when(core_ref[0] != 0)
    def _():
        store(slice(half, None), slice(0, half))


def prepare(core, prints, marks):
    shape = jax.ShapeDtypeStruct((DEPTH, prints.shape[0] // 2), BF16)
    return pl.pallas_call(
        prep_kernel,
        in_specs=[pl.BlockSpec(memory_space=pltpu.SMEM), VMEM, VMEM],
        out_specs=[VMEM, VMEM],
        out_shape=[shape, shape],
        compiler_params=params(),
        name="prepare",
    )(core, prints, marks)


def piece_scores(queries, query_norm, piece_ref):
    extra = piece_ref[BITS:, :].astype(F32)
    norm = extra[2:3] + extra[3:4] + extra[4:5]
    inter = jnp.dot(queries, piece_ref[:BITS, :], preferred_element_type=F32)
    inverse = 1.0 / ((query_norm + norm) - inter)
    return (inter * inverse) * SCALE


def piece_values(piece_ref):
    extra = piece_ref[BITS:, :].astype(F32)
    target = lax.broadcasted_iota(jnp.int32, (TARGETS, extra.shape[1]), 0)
    hit = target == extra[1:2].astype(jnp.int32)
    return jnp.where(hit, extra[0:1], 0.0).astype(BF16)


def add_piece(scores, top, piece_ref, num, den):
    expo = jnp.exp2(scores - top).astype(BF16)
    rounded = expo.astype(F32)
    for k in range(expo.shape[1] // 128):
        den = den + rounded[:, k * 128 : (k + 1) * 128]
    num = num + lax.dot_general(
        expo,
        piece_values(piece_ref),
        (((1,), (1,)), ((), ())),
        preferred_element_type=F32,
    )
    return num, den


def squared_norm(queries):
    wide = queries.astype(F32)
    return jnp.sum(wide * wide, axis=1, keepdims=True)


def unpack(state):
    num, marks = state[:, :TARGETS], state[:, TARGETS:]
    lane = lax.broadcasted_iota(jnp.int32, marks.shape, 1)
    return num, jnp.where(lane == 1, marks, 0.0), marks[:, 0:1], marks[:, 2:3]


def pack(num, den, top, weight):
    lane = lax.broadcasted_iota(jnp.int32, den.shape, 1)
    marks = jnp.where(lane == 0, top, jnp.sum(den, axis=1, keepdims=True))
    marks = jnp.where(lane == 2, weight, marks)
    return jnp.concatenate([num, marks], axis=1)


def empty(rows):
    return jnp.zeros((rows, TARGETS), F32), jnp.zeros((rows, 128), F32)


def add_pieces(queries_ref, state_in, state_ref, pieces, weight=None):
    queries = queries_ref[...]
    query_norm = squared_norm(queries)
    if state_in is None:
        num, den = empty(queries.shape[0])
        top = None
    else:
        num, den, top, weight = unpack(state_in[...])
    for piece_ref in pieces:
        scores = piece_scores(queries, query_norm, piece_ref)
        if top is None:
            top = jnp.max(scores, axis=1, keepdims=True) + MARGIN
        num, den = add_piece(scores, top, piece_ref, num, den)
    fits = jnp.max(den) <= 1.0

    @pl.when(fits)
    def _():
        state_ref[...] = pack(num, den, top, weight)

    @pl.when(jnp.logical_not(fits))
    def _():
        if state_in is None:
            state_ref[...] = pack(num, den, top, weight)

        @pl.loop(0, queries_ref.shape[0] // REDO)
        def _(block):
            here = pl.ds(pl.multiple_of(block * REDO, REDO), REDO)
            queries = queries_ref[here, :]
            query_norm = squared_norm(queries)
            best = jnp.zeros((REDO, 1), F32)
            for piece_ref in pieces:
                scores = piece_scores(queries, query_norm, piece_ref)
                best = jnp.maximum(best, jnp.max(scores, axis=1, keepdims=True))
            if state_in is None:
                top = best + MARGIN
                num, den = empty(REDO)
                weight = unpack(state_ref[here, :])[3]
            else:
                num, den, old, weight = unpack(state_in[here, :])
                top = jnp.maximum(old, best + MARGIN)
                scale = jnp.exp2(old - top)
                num, den = num * scale, den * scale
            for piece_ref in pieces:
                scores = piece_scores(queries, query_norm, piece_ref)
                num, den = add_piece(scores, top, piece_ref, num, den)
            state_ref[here, :] = pack(num, den, top, weight)


def first_kernel(queries_ref, weight_ref, *refs):
    columns = weight_ref[...].T
    weight = jnp.concatenate([columns[:, k : k + 1] for k in range(columns.shape[1])], axis=0)
    add_pieces(queries_ref, None, refs[-1], refs[:-1], weight)


def more_kernel(queries_ref, state_in, *refs):
    add_pieces(queries_ref, state_in, refs[-1], refs[:-1])


def split(value):
    high = value.astype(BF16)
    return high, (value - high.astype(F32)).astype(BF16)


def last_kernel(count, queries_ref, state_in, *refs):
    state_ref, moments_ref = refs[count:]
    add_pieces(queries_ref, state_in, state_ref, refs[:count])
    num, den, _, weight = unpack(state_ref[...])
    profile = num * (1.0 / jnp.sum(den, axis=1, keepdims=True))
    state_ref[:, :TARGETS] = profile
    weight_total = jnp.sum(weight, axis=0, keepdims=True)
    first = jnp.sum(profile * weight, axis=0, keepdims=True)
    mean = first / weight_total
    spread = (profile - mean) * jnp.sqrt(weight)
    outer = (((0,), (0,)), ((), ()))
    high, low = split(spread)
    cross = lax.dot_general(high, low, outer, preferred_element_type=F32)
    moments = lax.dot_general(high, high, outer, preferred_element_type=F32) + (cross + cross.T)
    moments = moments + lax.dot_general(
        mean, first, outer, precision=EXACT, preferred_element_type=F32
    )
    row = lax.broadcasted_iota(jnp.int32, (TARGETS, TARGETS), 0)
    column = lax.broadcasted_iota(jnp.int32, (TARGETS, TARGETS), 1)
    moments = jnp.where((row == 0) & (column > 0), first, moments)
    moments = jnp.where((row == 1) & (column == 2), first[0:1, 0:1], moments)
    moments = jnp.where((row == 1) & (column == 3), weight_total, moments)
    moments_ref[...] = moments


def work(rows, pieces):
    refs = sum(piece.shape[1] for piece in pieces)
    return cost(6 * rows * refs * (BITS + TARGETS), rows * 2048 + refs * DEPTH * 2)


def state_shape(rows):
    return jax.ShapeDtypeStruct((rows, TARGETS + 128), F32)


def first_part(queries, weight, pieces):
    rows = queries.shape[0]
    return pl.pallas_call(
        first_kernel,
        in_specs=[VMEM] * (2 + len(pieces)),
        out_specs=VMEM,
        out_shape=state_shape(rows),
        compiler_params=params(),
        cost_estimate=work(rows, pieces),
        name="first_part",
    )(queries, weight.reshape(rows // 128, 128), *pieces)


def more_part(queries, state, pieces):
    rows = queries.shape[0]
    return pl.pallas_call(
        more_kernel,
        in_specs=[VMEM] * (2 + len(pieces)),
        out_specs=VMEM,
        out_shape=state_shape(rows),
        input_output_aliases={1: 0},
        compiler_params=params(),
        cost_estimate=work(rows, pieces),
        name="more_part",
    )(queries, state, *pieces)


def last_part(queries, state, pieces):
    rows = queries.shape[0]
    return pl.pallas_call(
        functools.partial(last_kernel, len(pieces)),
        in_specs=[VMEM] * (2 + len(pieces)),
        out_specs=[VMEM] * 2,
        out_shape=[state_shape(rows), jax.ShapeDtypeStruct((TARGETS, TARGETS), F32)],
        input_output_aliases={1: 0},
        compiler_params=params(),
        cost_estimate=work(rows, pieces),
        name="last_part",
    )(queries, state, *pieces)


def repeat_row(block, at):
    return jnp.broadcast_to(block[at : at + 1, :], block.shape)


def inverse_factor(schur, size):
    groups = PANEL // 8
    panels = size // PANEL
    sub = lax.broadcasted_iota(jnp.int32, (8, 128), 0)
    eye = (
        lax.broadcasted_iota(jnp.int32, (PANEL, PANEL), 0)
        == lax.broadcasted_iota(jnp.int32, (PANEL, PANEL), 1)
    ).astype(F32)
    schur = [schur[i * PANEL : (i + 1) * PANEL, :] for i in range(panels)]
    inverse = [None] * panels
    result = []
    for t in range(panels):
        start = t * PANEL
        lane0 = start // 128 * 128
        left = schur[t][:, lane0:]
        right = [inverse[t]] if t else []
        right.append(eye)
        width = start + PANEL
        if width % 128:
            right.append(jnp.zeros((PANEL, -width % 128), F32))
        right = jnp.concatenate(right, axis=1)
        nl, nr = left.shape[1] // 128, right.shape[1] // 128
        tiles = [
            [left[8 * g : 8 * g + 8, 128 * k : 128 * k + 128] for k in range(nl)]
            + [right[8 * g : 8 * g + 8, 128 * k : 128 * k + 128] for k in range(nr)]
            for g in range(groups)
        ]
        square = left[:, start - lane0 : start - lane0 + PANEL]
        spread = [
            [
                jnp.broadcast_to(square[8 * g : 8 * g + 8, k : k + 1], (8, 128))
                if g >= k // 8
                else None
                for g in range(groups)
            ]
            for k in range(PANEL)
        ]
        inverses = []
        for k in range(PANEL):
            own, at = divmod(k, 8)
            inv = 1.0 / repeat_row(spread[k][own], at)
            inverses.append(inv)
            column = [
                spread[k][g] if g > own else jnp.where(sub > at, spread[k][g], 0.0) if g == own else None
                for g in range(groups)
            ]
            for m in range(k + 1, PANEL):
                factor = repeat_row(spread[k][m // 8], m % 8)
                for g in range(m // 8, groups):
                    spread[m][g] = spread[m][g] - (column[g] * factor) * inv
            multiple = [None if c is None else c * inv for c in column]
            for k2 in range(nl + nr):
                row = repeat_row(tiles[own][k2], at)
                for g in range(own, groups):
                    tiles[g][k2] = tiles[g][k2] - multiple[g] * row
        scale = []
        for g in range(groups):
            column = inverses[8 * g]
            for o in range(1, 8):
                column = jnp.where(sub == o, inverses[8 * g + o], column)
            scale.append(column)
        root = [jnp.sqrt(column) for column in scale]
        blank = [jnp.zeros((8, 128), F32)] * (size // 128 - nr)
        result.append(
            jnp.concatenate(
                [
                    jnp.concatenate([tiles[g][nl + k] * root[g] for k in range(nr)] + blank, axis=1)
                    for g in range(groups)
                ],
                axis=0,
            )
        )
        if t == panels - 1:
            break
        upper = jnp.concatenate([jnp.concatenate(tiles[g], axis=1) for g in range(groups)], axis=0)
        scaled = jnp.concatenate(
            [
                jnp.concatenate([tiles[g][k] * scale[g] for k in range(nl)], axis=1)
                for g in range(groups)
            ],
            axis=0,
        )
        for low, high in ((t + 1, t + 2), (t + 2, panels)):
            if low >= high:
                continue
            update = lax.dot_general(
                scaled[:, low * PANEL - lane0 : high * PANEL - lane0],
                upper,
                (((0,), (0,)), ((), ())),
                precision=EXACT,
                preferred_element_type=F32,
            )
            for i in range(low, high):
                part = update[(i - low) * PANEL : (i - low + 1) * PANEL]
                kept = [schur[i][:, :lane0]] if lane0 else []
                schur[i] = jnp.concatenate(kept + [schur[i][:, lane0:] - part[:, : nl * 128]], axis=1)
                fresh = -part[:, nl * 128 : nl * 128 + width]
                if inverse[i] is not None:
                    fresh = jnp.concatenate([inverse[i] + fresh[:, :start], fresh[:, start:]], axis=1)
                inverse[i] = fresh
    return jnp.concatenate(result, axis=0)


def whiten_kernel(moments_ref, state_ref, out_ref):
    total = moments_ref[...]
    row = lax.broadcasted_iota(jnp.int32, (TARGETS, TARGETS), 0)
    column = lax.broadcasted_iota(jnp.int32, (TARGETS, TARGETS), 1)
    share = 1.0 / total[1:2, 3:4]
    first = jnp.where(column[0:1] == 0, total[1:2, 2:3], total[0:1, :])
    mean = first * share
    outer = lax.dot_general(
        mean, mean, (((0,), (0,)), ((), ())), precision=EXACT, preferred_element_type=F32
    )
    lower = jnp.where(column <= row, total, 0.0)
    strict = jnp.where(column < row, total, 0.0)
    covariance = (lower + strict.T) * share - outer
    covariance = covariance + jnp.where(row == column, SHRINKAGE, 0.0)
    inverse = inverse_factor(covariance, TARGETS)
    profile, _, _, weight = unpack(state_ref[...])
    centered = split((profile - mean) * jnp.sqrt(weight))
    inverse = split(inverse)

    def product(a, b):
        return lax.dot_general(a, b, (((1,), (1,)), ((), ())), preferred_element_type=F32)

    cross = product(centered[0], inverse[1]) + product(centered[1], inverse[0])
    out_ref[...] = product(centered[0], inverse[0]) + cross


def whiten(moments, state):
    return pl.pallas_call(
        whiten_kernel,
        in_specs=[VMEM, VMEM],
        out_specs=VMEM,
        out_shape=jax.ShapeDtypeStruct((state.shape[0], TARGETS), F32),
        compiler_params=params(),
        name="whiten",
    )(moments, state)


def all_sum(moments):
    plane, line = lax.axis_size(PLANE), lax.axis_size("z")
    rows = TARGETS // plane
    parts = lax.all_to_all(moments.reshape(plane, rows, TARGETS), PLANE, 0, 0)
    part = jnp.sum(parts, axis=0, keepdims=True)
    parts = lax.all_to_all(jnp.broadcast_to(part, (line, rows, TARGETS)), "z", 0, 0)
    part = jnp.sum(parts, axis=0, keepdims=True)
    parts = lax.all_to_all(jnp.broadcast_to(part, (plane, rows, TARGETS)), PLANE, 0, 0)
    return parts.reshape(TARGETS, TARGETS)


def on_device(compounds, compound_weight, reference_prints, potency, target_label):
    core = lax.axis_index("core").astype(jnp.int32).reshape(1)
    marks = target_label.astype(F32) * 16.0 + potency.astype(F32)
    mine, other = prepare(core, reference_prints, marks[None, :])

    hold = lax.optimization_barrier
    beside, flipped, rest = send(mine, onward), send(mine, flip), send(other, onward)
    far, flipped_far = send(beside, onward), send(beside, across)
    ahead, ahead_rest = send(flipped, onward), send(rest, flip)
    near = [beside, flipped, rest]
    near += [send(piece, sibling) for piece in near]
    state = first_part(compounds, compound_weight, [mine, other] + near)
    far, flipped_far, ahead, ahead_rest, state = hold((far, flipped_far, ahead, ahead_rest, state))
    last = [far, flipped_far, ahead, ahead_rest]
    others = [send(piece, sibling) for piece in last]
    state = more_part(compounds, state, last)
    state, moments = last_part(compounds, state, others)
    return whiten(all_sum(moments), state)


def solution(mesh):
    sizes = dict(core=2, x_lo=2, x_hi=2)
    sizes["z"] = mesh.shape["lib"] // (sizes["core"] * sizes["x_lo"])
    sizes["y"] = mesh.shape["ref"] // sizes["x_hi"]
    fine = jax.sharding.Mesh(mesh.devices.reshape([sizes[name] for name in ALL]), ALL)
    spread = ALL
    across_refs = ("y", "x_hi")
    placed = (P(spread, None), P(spread), P(across_refs, None), P(across_refs), P(across_refs))
    return jax.shard_map(
        on_device, mesh=fine, in_specs=placed, out_specs=P(spread, None), check_vma=False
    )
```

```python
import functools

import jax
import jax.numpy as jnp
from jax import lax
from jax.experimental import pallas as pl
from jax.experimental.pallas import tpu as pltpu
from jax.sharding import PartitionSpec as P

ALL = ("z", "x_lo", "core", "y", "x_hi")
PLANE = ("x_lo", "core", "y", "x_hi")
BITS = 512
EXTRA = 16
DEPTH = BITS + EXTRA
TARGETS = 256
SHRINKAGE = 0.02
LOG2E = 1.4426950408889634
SCALE = 320.0 * LOG2E
MARGIN = 58.0
PANEL = 32
SPREAD = 16
REDO = 128
F32 = jnp.float32
BF16 = jnp.bfloat16
EXACT = lax.Precision.HIGHEST
VMEM = pl.BlockSpec(memory_space=pltpu.VMEM)


def params(mib=20):
    return pltpu.CompilerParams(vmem_limit_bytes=mib * 2**20)


def cost(flops, size):
    return pl.CostEstimate(flops=flops, bytes_accessed=size, transcendentals=0)


def place(x, y, z, c):
    return ((z % 8 * 2 + x % 2) * 2 + c % 2) * 8 + y % 4 * 2 + x // 2


def route(move):
    pairs = []
    for x in range(4):
        for y in range(4):
            for z in range(8):
                for c in range(2):
                    pairs.append((place(x, y, z, c), place(*move(x, y, z, c))))
    return sorted(pairs)


def send(value, move):
    return lax.ppermute(value, ALL, route(move))


def flip(x, y, z, c):
    return 3 - x, y, z, c


def onward(x, y, z, c):
    return x, y + 1 - 2 * c, z, c


def across(x, y, z, c):
    return 3 - x, y + 1 - 2 * c, z, c


def sibling(x, y, z, c):
    return x, y, z, 1 - c


def prep_kernel(core_ref, prints_ref, marks_ref, mine_ref, other_ref):
    prints = prints_ref[...].T
    wide = prints.astype(F32)
    norm = jnp.sum(wide * wide, axis=0, keepdims=True)
    high = norm.astype(BF16)
    rest = norm - high.astype(F32)
    middle = rest.astype(BF16)
    low = (rest - middle.astype(F32)).astype(BF16)
    marks = marks_ref[...]
    label = jnp.floor(marks * (1.0 / 16.0))
    row = lax.broadcasted_iota(jnp.int32, (EXTRA, prints.shape[1]), 0)
    extra = jnp.where(row == 0, marks - 16.0 * label, 0.0)
    extra = jnp.where(row == 1, label, extra)
    for at, part in ((2, high), (3, middle), (4, low)):
        extra = jnp.where(row == at, part.astype(F32), extra)
    extra = extra.astype(BF16)
    half = prints.shape[1] // 2

    def store(mine, other):
        for ref, part in ((mine_ref, mine), (other_ref, other)):
            ref[:BITS, :] = prints[:, part]
            ref[BITS:, :] = extra[:, part]

    @pl.when(core_ref[0] == 0)
    def _():
        store(slice(0, half), slice(half, None))

    @pl.when(core_ref[0] != 0)
    def _():
        store(slice(half, None), slice(0, half))


def prepare(core, prints, marks):
    shape = jax.ShapeDtypeStruct((DEPTH, prints.shape[0] // 2), BF16)
    return pl.pallas_call(
        prep_kernel,
        in_specs=[pl.BlockSpec(memory_space=pltpu.SMEM), VMEM, VMEM],
        out_specs=[VMEM, VMEM],
        out_shape=[shape, shape],
        compiler_params=params(),
        name="prepare",
    )(core, prints, marks)


def piece_scores(queries, query_norm, piece_ref):
    extra = piece_ref[BITS:, :].astype(F32)
    norm = extra[2:3] + extra[3:4] + extra[4:5]
    inter = jnp.dot(queries, piece_ref[:BITS, :], preferred_element_type=F32)
    inverse = 1.0 / ((query_norm + norm) - inter)
    return (inter * inverse) * SCALE


def piece_values(piece_ref):
    extra = piece_ref[BITS:, :].astype(F32)
    target = lax.broadcasted_iota(jnp.int32, (TARGETS, extra.shape[1]), 0)
    hit = target == extra[1:2].astype(jnp.int32)
    return jnp.where(hit, extra[0:1], 0.0).astype(BF16)


def add_piece(scores, top, piece_ref, num, den):
    expo = jnp.exp2(scores - top).astype(BF16)
    rounded = expo.astype(F32)
    for k in range(expo.shape[1] // 128):
        den = den + rounded[:, k * 128 : (k + 1) * 128]
    num = num + lax.dot_general(
        expo,
        piece_values(piece_ref),
        (((1,), (1,)), ((), ())),
        preferred_element_type=F32,
    )
    return num, den


def squared_norm(queries):
    wide = queries.astype(F32)
    return jnp.sum(wide * wide, axis=1, keepdims=True)


def unpack(state):
    num, marks = state[:, :TARGETS], state[:, TARGETS:]
    lane = lax.broadcasted_iota(jnp.int32, marks.shape, 1)
    return num, jnp.where(lane == 1, marks, 0.0), marks[:, 0:1], marks[:, 2:3]


def pack(num, den, top, weight):
    lane = lax.broadcasted_iota(jnp.int32, den.shape, 1)
    marks = jnp.where(lane == 0, top, jnp.sum(den, axis=1, keepdims=True))
    marks = jnp.where(lane == 2, weight, marks)
    return jnp.concatenate([num, marks], axis=1)


def empty(rows):
    return jnp.zeros((rows, TARGETS), F32), jnp.zeros((rows, 128), F32)


def add_pieces(queries_ref, state_in, state_ref, pieces, weight=None):
    queries = queries_ref[...]
    query_norm = squared_norm(queries)
    if state_in is None:
        num, den = empty(queries.shape[0])
        top = None
    else:
        num, den, top, weight = unpack(state_in[...])
    for piece_ref in pieces:
        scores = piece_scores(queries, query_norm, piece_ref)
        if top is None:
            top = jnp.max(scores, axis=1, keepdims=True) + MARGIN
        num, den = add_piece(scores, top, piece_ref, num, den)
    fits = jnp.max(den) <= 1.0

    @pl.when(fits)
    def _():
        state_ref[...] = pack(num, den, top, weight)

    @pl.when(jnp.logical_not(fits))
    def _():
        if state_in is None:
            state_ref[...] = pack(num, den, top, weight)

        @pl.loop(0, queries_ref.shape[0] // REDO)
        def _(block):
            here = pl.ds(pl.multiple_of(block * REDO, REDO), REDO)
            queries = queries_ref[here, :]
            query_norm = squared_norm(queries)
            best = jnp.zeros((REDO, 1), F32)
            for piece_ref in pieces:
                scores = piece_scores(queries, query_norm, piece_ref)
                best = jnp.maximum(best, jnp.max(scores, axis=1, keepdims=True))
            if state_in is None:
                top = best + MARGIN
                num, den = empty(REDO)
                weight = unpack(state_ref[here, :])[3]
            else:
                num, den, old, weight = unpack(state_in[here, :])
                top = jnp.maximum(old, best + MARGIN)
                scale = jnp.exp2(old - top)
                num, den = num * scale, den * scale
            for piece_ref in pieces:
                scores = piece_scores(queries, query_norm, piece_ref)
                num, den = add_piece(scores, top, piece_ref, num, den)
            state_ref[here, :] = pack(num, den, top, weight)


def first_kernel(queries_ref, weight_ref, *refs):
    columns = weight_ref[...].T
    weight = jnp.concatenate([columns[:, k : k + 1] for k in range(columns.shape[1])], axis=0)
    add_pieces(queries_ref, None, refs[-1], refs[:-1], weight)


def more_kernel(queries_ref, state_in, *refs):
    add_pieces(queries_ref, state_in, refs[-1], refs[:-1])


def split(value):
    high = value.astype(BF16)
    return high, (value - high.astype(F32)).astype(BF16)


def last_kernel(count, queries_ref, state_in, *refs):
    state_ref, moments_ref = refs[count:]
    add_pieces(queries_ref, state_in, state_ref, refs[:count])
    num, den, _, weight = unpack(state_ref[...])
    profile = num * (1.0 / jnp.sum(den, axis=1, keepdims=True))
    state_ref[:, :TARGETS] = profile
    weight_total = jnp.sum(weight, axis=0, keepdims=True)
    first = jnp.sum(profile * weight, axis=0, keepdims=True)
    mean = first / weight_total
    spread = (profile - mean) * jnp.sqrt(weight)
    outer = (((0,), (0,)), ((), ()))
    high, low = split(spread)
    cross = lax.dot_general(high, low, outer, preferred_element_type=F32)
    moments = lax.dot_general(high, high, outer, preferred_element_type=F32) + (cross + cross.T)
    moments = moments + lax.dot_general(
        mean, first, outer, precision=EXACT, preferred_element_type=F32
    )
    row = lax.broadcasted_iota(jnp.int32, (TARGETS, TARGETS), 0)
    column = lax.broadcasted_iota(jnp.int32, (TARGETS, TARGETS), 1)
    moments = jnp.where((row == 0) & (column > 0), first, moments)
    moments = jnp.where((row == 1) & (column == 2), first[0:1, 0:1], moments)
    moments = jnp.where((row == 1) & (column == 3), weight_total, moments)
    moments_ref[...] = moments


def work(rows, pieces):
    refs = sum(piece.shape[1] for piece in pieces)
    return cost(6 * rows * refs * (BITS + TARGETS), rows * 2048 + refs * DEPTH * 2)


def state_shape(rows):
    return jax.ShapeDtypeStruct((rows, TARGETS + 128), F32)


def first_part(queries, weight, pieces):
    rows = queries.shape[0]
    return pl.pallas_call(
        first_kernel,
        in_specs=[VMEM] * (2 + len(pieces)),
        out_specs=VMEM,
        out_shape=state_shape(rows),
        compiler_params=params(),
        cost_estimate=work(rows, pieces),
        name="first_part",
    )(queries, weight.reshape(rows // 128, 128), *pieces)


def more_part(queries, state, pieces):
    rows = queries.shape[0]
    return pl.pallas_call(
        more_kernel,
        in_specs=[VMEM] * (2 + len(pieces)),
        out_specs=VMEM,
        out_shape=state_shape(rows),
        input_output_aliases={1: 0},
        compiler_params=params(),
        cost_estimate=work(rows, pieces),
        name="more_part",
    )(queries, state, *pieces)


def last_part(queries, state, pieces):
    rows = queries.shape[0]
    return pl.pallas_call(
        functools.partial(last_kernel, len(pieces)),
        in_specs=[VMEM] * (2 + len(pieces)),
        out_specs=[VMEM] * 2,
        out_shape=[state_shape(rows), jax.ShapeDtypeStruct((TARGETS, TARGETS), F32)],
        input_output_aliases={1: 0},
        compiler_params=params(),
        cost_estimate=work(rows, pieces),
        name="last_part",
    )(queries, state, *pieces)


def repeat_row(block, at):
    return jnp.broadcast_to(block[at : at + 1, :], block.shape)


def three_way(value):
    high = value.astype(BF16)
    rest = value - high.astype(F32)
    middle = rest.astype(BF16)
    return high, middle, (rest - middle.astype(F32)).astype(BF16)


def exact_outer(a, b):
    a0, a1, a2 = three_way(a)
    b0, b1, b2 = three_way(b)
    left = jnp.concatenate([a2, a0, a1, a1, a0, a0], axis=0)
    right = jnp.concatenate([b0, b2, b1, b0, b1, b0], axis=0)
    return lax.dot_general(left, right, (((0,), (0,)), ((), ())), preferred_element_type=F32)


def eliminate(tiles, square, sub):
    groups, pivots = len(tiles), []
    at_tile, at_lane = divmod(square, 128)
    for base in range(0, PANEL, SPREAD):
        columns = [
            {
                g: jnp.broadcast_to(tiles[g][at_tile][:, lane : lane + 1], (8, 128))
                for g in range((base + k) // 8, groups)
            }
            for k, lane in enumerate(range(at_lane + base, at_lane + base + SPREAD))
        ]
        for k in range(0, SPREAD, 2):
            own, at = divmod(base + k, 8)
            first, second = columns[k], columns[k + 1]
            a, b = repeat_row(first[own], at), repeat_row(first[own], at + 1)
            c = repeat_row(second[own], at + 1)
            inverse0 = 1.0 / a
            inverse1 = a * (1.0 / (a * c - b * b))
            pivots += [inverse0, inverse1]
            below = range(own, groups)
            first_low = {g: jnp.where(sub > at, first[g], 0.0) if g == own else first[g] for g in below}
            multiple0 = {g: first_low[g] * inverse0 for g in below}
            second_low = {g: second[g] - multiple0[g] * b for g in below}
            second_low[own] = jnp.where(sub > at + 1, second_low[own], 0.0)
            multiple1 = {g: second_low[g] * inverse1 for g in below}
            for m in range(k + 2, SPREAD):
                group, row = divmod(base + m, 8)
                factor0 = repeat_row(first[group], row)
                factor1 = repeat_row(second_low[group], row)
                for g in columns[m]:
                    if m < k + 4:
                        step = (second_low[g] * factor1) * inverse1
                        columns[m][g] = (columns[m][g] - multiple0[g] * factor0) - step
                    else:
                        step = multiple0[g] * factor0 + multiple1[g] * factor1
                        columns[m][g] = columns[m][g] - step
            for t in range(len(tiles[own])):
                for multiple, row in ((multiple0, at), (multiple1, at + 1)):
                    factor = repeat_row(tiles[own][t], row)
                    for g in below:
                        tiles[g][t] = tiles[g][t] - multiple[g] * factor
    return pivots


def inverse_factor(schur, size):
    groups, panels = PANEL // 8, size // PANEL
    sub = lax.broadcasted_iota(jnp.int32, (8, 128), 0)
    eye = (
        lax.broadcasted_iota(jnp.int32, (PANEL, PANEL), 0)
        == lax.broadcasted_iota(jnp.int32, (PANEL, PANEL), 1)
    ).astype(F32)
    schur = [schur[i * PANEL : (i + 1) * PANEL, :] for i in range(panels)]
    inverse = [None] * panels
    result = []
    for t in range(panels):
        start = t * PANEL
        lane0 = start // 128 * 128
        left = schur[t][:, lane0:]
        right = [inverse[t]] if t else []
        right.append(eye)
        width = start + PANEL
        if width % 128:
            right.append(jnp.zeros((PANEL, -width % 128), F32))
        right = jnp.concatenate(right, axis=1)
        nl, nr = left.shape[1] // 128, right.shape[1] // 128
        tiles = [
            [left[8 * g : 8 * g + 8, 128 * k : 128 * k + 128] for k in range(nl)]
            + [right[8 * g : 8 * g + 8, 128 * k : 128 * k + 128] for k in range(nr)]
            for g in range(groups)
        ]
        inverses = eliminate(tiles, start - lane0, sub)
        scale = []
        for g in range(groups):
            column = inverses[8 * g]
            for o in range(1, 8):
                column = jnp.where(sub == o, inverses[8 * g + o], column)
            scale.append(column)
        root = [jnp.sqrt(column) for column in scale]
        blank = [jnp.zeros((8, 128), F32)] * (size // 128 - nr)
        result.append(
            jnp.concatenate(
                [
                    jnp.concatenate([tiles[g][nl + k] * root[g] for k in range(nr)] + blank, axis=1)
                    for g in range(groups)
                ],
                axis=0,
            )
        )
        if t == panels - 1:
            break
        upper = jnp.concatenate([jnp.concatenate(tiles[g], axis=1) for g in range(groups)], axis=0)
        scaled = jnp.concatenate(
            [
                jnp.concatenate([tiles[g][k] * scale[g] for k in range(nl)], axis=1)
                for g in range(groups)
            ],
            axis=0,
        )
        for low, high in ((t + 1, t + 2), (t + 2, panels)):
            if low >= high:
                continue
            update = exact_outer(scaled[:, low * PANEL - lane0 : high * PANEL - lane0], upper)
            for i in range(low, high):
                part = update[(i - low) * PANEL : (i - low + 1) * PANEL]
                kept = [schur[i][:, :lane0]] if lane0 else []
                schur[i] = jnp.concatenate(kept + [schur[i][:, lane0:] - part[:, : nl * 128]], axis=1)
                fresh = -part[:, nl * 128 : nl * 128 + width]
                if inverse[i] is not None:
                    fresh = jnp.concatenate([inverse[i] + fresh[:, :start], fresh[:, start:]], axis=1)
                inverse[i] = fresh
    return jnp.concatenate(result, axis=0)


def whiten_kernel(moments_ref, state_ref, out_ref):
    total = moments_ref[...]
    row = lax.broadcasted_iota(jnp.int32, (TARGETS, TARGETS), 0)
    column = lax.broadcasted_iota(jnp.int32, (TARGETS, TARGETS), 1)
    share = 1.0 / total[1:2, 3:4]
    first = jnp.where(column[0:1] == 0, total[1:2, 2:3], total[0:1, :])
    mean = first * share
    outer = lax.dot_general(
        mean, mean, (((0,), (0,)), ((), ())), precision=EXACT, preferred_element_type=F32
    )
    lower = jnp.where(column <= row, total, 0.0)
    strict = jnp.where(column < row, total, 0.0)
    covariance = (lower + strict.T) * share - outer
    covariance = covariance + jnp.where(row == column, SHRINKAGE, 0.0)
    inverse = inverse_factor(covariance, TARGETS)
    profile, _, _, weight = unpack(state_ref[...])
    centered = split((profile - mean) * jnp.sqrt(weight))
    inverse = split(inverse)

    def product(a, b):
        return lax.dot_general(a, b, (((1,), (1,)), ((), ())), preferred_element_type=F32)

    cross = product(centered[0], inverse[1]) + product(centered[1], inverse[0])
    out_ref[...] = product(centered[0], inverse[0]) + cross


def whiten(moments, state):
    return pl.pallas_call(
        whiten_kernel,
        in_specs=[VMEM, VMEM],
        out_specs=VMEM,
        out_shape=jax.ShapeDtypeStruct((state.shape[0], TARGETS), F32),
        compiler_params=params(),
        name="whiten",
    )(moments, state)


def all_sum(moments):
    plane, line = lax.axis_size(PLANE), lax.axis_size("z")
    rows = TARGETS // plane
    parts = lax.all_to_all(moments.reshape(plane, rows, TARGETS), PLANE, 0, 0)
    part = jnp.sum(parts, axis=0, keepdims=True)
    parts = lax.all_to_all(jnp.broadcast_to(part, (line, rows, TARGETS)), "z", 0, 0)
    part = jnp.sum(parts, axis=0, keepdims=True)
    parts = lax.all_to_all(jnp.broadcast_to(part, (plane, rows, TARGETS)), PLANE, 0, 0)
    return parts.reshape(TARGETS, TARGETS)


def on_device(compounds, compound_weight, reference_prints, potency, target_label):
    core = lax.axis_index("core").astype(jnp.int32).reshape(1)
    marks = target_label.astype(F32) * 16.0 + potency.astype(F32)
    mine, other = prepare(core, reference_prints, marks[None, :])

    hold = lax.optimization_barrier
    beside, flipped, rest = send(mine, onward), send(mine, flip), send(other, onward)
    far, flipped_far = send(beside, onward), send(beside, across)
    ahead, ahead_rest = send(flipped, onward), send(rest, flip)
    near = [beside, flipped, rest]
    near += [send(piece, sibling) for piece in near]
    state = first_part(compounds, compound_weight, [mine, other] + near)
    far, flipped_far, ahead, ahead_rest, state = hold((far, flipped_far, ahead, ahead_rest, state))
    last = [far, flipped_far, ahead, ahead_rest]
    others = [send(piece, sibling) for piece in last]
    state = more_part(compounds, state, last)
    state, moments = last_part(compounds, state, others)
    return whiten(all_sum(moments), state)


def solution(mesh):
    sizes = dict(core=2, x_lo=2, x_hi=2)
    sizes["z"] = mesh.shape["lib"] // (sizes["core"] * sizes["x_lo"])
    sizes["y"] = mesh.shape["ref"] // sizes["x_hi"]
    fine = jax.sharding.Mesh(mesh.devices.reshape([sizes[name] for name in ALL]), ALL)
    spread = ALL
    across_refs = ("y", "x_hi")
    placed = (P(spread, None), P(spread), P(across_refs, None), P(across_refs), P(across_refs))
    return jax.shard_map(
        on_device, mesh=fine, in_specs=placed, out_specs=P(spread, None), check_vma=False
    )
```

```python
import functools

import jax
import jax.numpy as jnp
from jax import lax
from jax.experimental import pallas as pl
from jax.experimental.pallas import tpu as pltpu
from jax.sharding import PartitionSpec as P

ALL = ("z", "x_lo", "core", "y", "x_hi")
PLANE = ("x_lo", "core", "y", "x_hi")
BITS = 512
EXTRA = 16
DEPTH = BITS + EXTRA
TARGETS = 256
SHRINKAGE = 0.02
LOG2E = 1.4426950408889634
SCALE = 320.0 * LOG2E
MARGIN = 58.0
PANEL = 32
SPREAD = 16
REDO = 128
F32 = jnp.float32
BF16 = jnp.bfloat16
EXACT = lax.Precision.HIGHEST
VMEM = pl.BlockSpec(memory_space=pltpu.VMEM)


def params(mib=20):
    return pltpu.CompilerParams(vmem_limit_bytes=mib * 2**20)


def cost(flops, size):
    return pl.CostEstimate(flops=flops, bytes_accessed=size, transcendentals=0)


def place(x, y, z, c):
    return ((z % 8 * 2 + x % 2) * 2 + c % 2) * 8 + y % 4 * 2 + x // 2


def route(move):
    pairs = []
    for x in range(4):
        for y in range(4):
            for z in range(8):
                for c in range(2):
                    pairs.append((place(x, y, z, c), place(*move(x, y, z, c))))
    return sorted(pairs)


def send(value, move):
    return lax.ppermute(value, ALL, route(move))


def flip(x, y, z, c):
    return 3 - x, y, z, c


def onward(x, y, z, c):
    return x, y + 1 - 2 * c, z, c


def across(x, y, z, c):
    return 3 - x, y + 1 - 2 * c, z, c


def sibling(x, y, z, c):
    return x, y, z, 1 - c


def prep_kernel(core_ref, prints_ref, marks_ref, mine_ref, other_ref):
    prints = prints_ref[...].T
    wide = prints.astype(F32)
    norm = jnp.sum(wide * wide, axis=0, keepdims=True)
    high = norm.astype(BF16)
    rest = norm - high.astype(F32)
    middle = rest.astype(BF16)
    low = (rest - middle.astype(F32)).astype(BF16)
    marks = marks_ref[...]
    label = jnp.floor(marks * (1.0 / 16.0))
    row = lax.broadcasted_iota(jnp.int32, (EXTRA, prints.shape[1]), 0)
    extra = jnp.where(row == 0, marks - 16.0 * label, 0.0)
    extra = jnp.where(row == 1, label, extra)
    for at, part in ((2, high), (3, middle), (4, low)):
        extra = jnp.where(row == at, part.astype(F32), extra)
    extra = extra.astype(BF16)
    half = prints.shape[1] // 2

    def store(mine, other):
        for ref, part in ((mine_ref, mine), (other_ref, other)):
            ref[:BITS, :] = prints[:, part]
            ref[BITS:, :] = extra[:, part]

    @pl.when(core_ref[0] == 0)
    def _():
        store(slice(0, half), slice(half, None))

    @pl.when(core_ref[0] != 0)
    def _():
        store(slice(half, None), slice(0, half))


def prepare(core, prints, marks):
    shape = jax.ShapeDtypeStruct((DEPTH, prints.shape[0] // 2), BF16)
    return pl.pallas_call(
        prep_kernel,
        in_specs=[pl.BlockSpec(memory_space=pltpu.SMEM), VMEM, VMEM],
        out_specs=[VMEM, VMEM],
        out_shape=[shape, shape],
        compiler_params=params(),
        name="prepare",
    )(core, prints, marks)


def piece_scores(queries, query_norm, piece_ref):
    extra = piece_ref[BITS:, :].astype(F32)
    norm = extra[2:3] + extra[3:4] + extra[4:5]
    inter = jnp.dot(queries, piece_ref[:BITS, :], preferred_element_type=F32)
    inverse = 1.0 / ((query_norm + norm) - inter)
    return (inter * inverse) * SCALE


def piece_values(piece_ref):
    extra = piece_ref[BITS:, :].astype(F32)
    target = lax.broadcasted_iota(jnp.int32, (TARGETS, extra.shape[1]), 0)
    hit = target == extra[1:2].astype(jnp.int32)
    return jnp.where(hit, extra[0:1], 0.0).astype(BF16)


def add_piece(scores, top, piece_ref, num, den):
    expo = jnp.exp2(scores - top).astype(BF16)
    rounded = expo.astype(F32)
    tiles = [rounded[:, k : k + 128] for k in range(0, rounded.shape[1], 128)]
    den = den + functools.reduce(jnp.add, tiles)
    num = num + lax.dot_general(
        expo,
        piece_values(piece_ref),
        (((1,), (1,)), ((), ())),
        preferred_element_type=F32,
    )
    return num, den


def squared_norm(queries):
    wide = queries.astype(F32)
    return jnp.sum(wide * wide, axis=1, keepdims=True)


def unpack(state):
    num, marks = state[:, :TARGETS], state[:, TARGETS:]
    lane = lax.broadcasted_iota(jnp.int32, marks.shape, 1)
    return num, jnp.where(lane == 1, marks, 0.0), marks[:, 0:1], marks[:, 2:3]


def pack(num, den, top, weight):
    lane = lax.broadcasted_iota(jnp.int32, den.shape, 1)
    marks = jnp.where(lane == 0, top, jnp.sum(den, axis=1, keepdims=True))
    marks = jnp.where(lane == 2, weight, marks)
    return jnp.concatenate([num, marks], axis=1)


def empty(rows):
    return jnp.zeros((rows, TARGETS), F32), jnp.zeros((rows, 128), F32)


def add_pieces(queries_ref, state_in, state_ref, pieces, weight=None, finish=False):
    queries = queries_ref[...]
    query_norm = squared_norm(queries)
    if state_in is None:
        num, den = empty(queries.shape[0])
        top = None
    else:
        num, den, top, weight = unpack(state_in[...])
    for piece_ref in pieces:
        scores = piece_scores(queries, query_norm, piece_ref)
        if top is None:
            top = jnp.max(scores, axis=1, keepdims=True) + MARGIN
        num, den = add_piece(scores, top, piece_ref, num, den)
    fits = jnp.max(den) <= 1.0

    def store(rows, num, den, top, weight):
        if finish:
            num = num * (1.0 / jnp.sum(den, axis=1, keepdims=True))
        state_ref[rows, :] = pack(num, den, top, weight)

    @pl.when(fits)
    def _():
        store(slice(None), num, den, top, weight)

    @pl.when(jnp.logical_not(fits))
    def _():
        if state_in is None:
            state_ref[...] = pack(num, den, top, weight)

        @pl.loop(0, queries_ref.shape[0] // REDO)
        def _(block):
            here = pl.ds(pl.multiple_of(block * REDO, REDO), REDO)
            queries = queries_ref[here, :]
            query_norm = squared_norm(queries)
            best = jnp.zeros((REDO, 1), F32)
            for piece_ref in pieces:
                scores = piece_scores(queries, query_norm, piece_ref)
                best = jnp.maximum(best, jnp.max(scores, axis=1, keepdims=True))
            if state_in is None:
                top = best + MARGIN
                num, den = empty(REDO)
                weight = unpack(state_ref[here, :])[3]
            else:
                num, den, old, weight = unpack(state_in[here, :])
                top = jnp.maximum(old, best + MARGIN)
                scale = jnp.exp2(old - top)
                num, den = num * scale, den * scale
            for piece_ref in pieces:
                scores = piece_scores(queries, query_norm, piece_ref)
                num, den = add_piece(scores, top, piece_ref, num, den)
            store(here, num, den, top, weight)


def first_kernel(queries_ref, weight_ref, *refs):
    columns = weight_ref[...].T
    weight = jnp.concatenate([columns[:, k : k + 1] for k in range(columns.shape[1])], axis=0)
    add_pieces(queries_ref, None, refs[-1], refs[:-1], weight)


def more_kernel(queries_ref, state_in, *refs):
    add_pieces(queries_ref, state_in, refs[-1], refs[:-1])


def split(value):
    high = value.astype(BF16)
    return high, (value - high.astype(F32)).astype(BF16)


def last_kernel(count, queries_ref, state_in, *refs):
    state_ref, moments_ref = refs[count:]
    add_pieces(queries_ref, state_in, state_ref, refs[:count], finish=True)
    profile, _, _, weight = unpack(state_ref[...])
    weight_total = jnp.sum(weight, axis=0, keepdims=True)
    first = jnp.sum(profile * weight, axis=0, keepdims=True)
    mean = first / weight_total
    spread = (profile - mean) * jnp.sqrt(weight)
    outer = (((0,), (0,)), ((), ()))
    high, low = split(spread)
    cross = lax.dot_general(high, low, outer, preferred_element_type=F32)
    moments = lax.dot_general(high, high, outer, preferred_element_type=F32) + (cross + cross.T)
    moments = moments + lax.dot_general(
        mean, first, outer, precision=EXACT, preferred_element_type=F32
    )
    row = lax.broadcasted_iota(jnp.int32, (TARGETS, TARGETS), 0)
    column = lax.broadcasted_iota(jnp.int32, (TARGETS, TARGETS), 1)
    moments = jnp.where((row == 0) & (column > 0), first, moments)
    moments = jnp.where((row == 1) & (column == 2), first[0:1, 0:1], moments)
    moments = jnp.where((row == 1) & (column == 3), weight_total, moments)
    moments_ref[...] = moments


def work(rows, pieces):
    refs = sum(piece.shape[1] for piece in pieces)
    return cost(6 * rows * refs * (BITS + TARGETS), rows * 2048 + refs * DEPTH * 2)


def state_shape(rows):
    return jax.ShapeDtypeStruct((rows, TARGETS + 128), F32)


def first_part(queries, weight, pieces):
    rows = queries.shape[0]
    return pl.pallas_call(
        first_kernel,
        in_specs=[VMEM] * (2 + len(pieces)),
        out_specs=VMEM,
        out_shape=state_shape(rows),
        compiler_params=params(),
        cost_estimate=work(rows, pieces),
        name="first_part",
    )(queries, weight.reshape(rows // 128, 128), *pieces)


def more_part(queries, state, pieces):
    rows = queries.shape[0]
    return pl.pallas_call(
        more_kernel,
        in_specs=[VMEM] * (2 + len(pieces)),
        out_specs=VMEM,
        out_shape=state_shape(rows),
        input_output_aliases={1: 0},
        compiler_params=params(),
        cost_estimate=work(rows, pieces),
        name="more_part",
    )(queries, state, *pieces)


def last_part(queries, state, pieces):
    rows = queries.shape[0]
    return pl.pallas_call(
        functools.partial(last_kernel, len(pieces)),
        in_specs=[VMEM] * (2 + len(pieces)),
        out_specs=[VMEM] * 2,
        out_shape=[state_shape(rows), jax.ShapeDtypeStruct((TARGETS, TARGETS), F32)],
        input_output_aliases={1: 0},
        compiler_params=params(),
        cost_estimate=work(rows, pieces),
        name="last_part",
    )(queries, state, *pieces)


def repeat_row(block, at):
    return jnp.broadcast_to(block[at : at + 1, :], block.shape)


def three_way(value):
    high = value.astype(BF16)
    rest = value - high.astype(F32)
    middle = rest.astype(BF16)
    return high, middle, (rest - middle.astype(F32)).astype(BF16)


def exact_outer(a, b):
    a0, a1, a2 = three_way(a)
    b0, b1, b2 = three_way(b)
    left = jnp.concatenate([a2, a0, a1, a1, a0, a0], axis=0)
    right = jnp.concatenate([b0, b2, b1, b0, b1, b0], axis=0)
    return lax.dot_general(left, right, (((0,), (0,)), ((), ())), preferred_element_type=F32)


def eliminate(tiles, square, sub):
    groups, pivots = len(tiles), []
    at_tile, at_lane = divmod(square, 128)
    for base in range(0, PANEL, SPREAD):
        columns = [
            {
                g: jnp.broadcast_to(tiles[g][at_tile][:, lane : lane + 1], (8, 128))
                for g in range((base + k) // 8, groups)
            }
            for k, lane in enumerate(range(at_lane + base, at_lane + base + SPREAD))
        ]
        for k in range(0, SPREAD, 2):
            own, at = divmod(base + k, 8)
            first, second = columns[k], columns[k + 1]
            a, b = repeat_row(first[own], at), repeat_row(first[own], at + 1)
            c = repeat_row(second[own], at + 1)
            inverse0 = 1.0 / a
            inverse1 = a * (1.0 / (a * c - b * b))
            pivots += [inverse0, inverse1]
            below = range(own, groups)
            first_low = {g: jnp.where(sub > at, first[g], 0.0) if g == own else first[g] for g in below}
            multiple0 = {g: first_low[g] * inverse0 for g in below}
            second_low = {g: second[g] - multiple0[g] * b for g in below}
            second_low[own] = jnp.where(sub > at + 1, second_low[own], 0.0)
            multiple1 = {g: second_low[g] * inverse1 for g in below}
            for m in range(k + 2, SPREAD):
                group, row = divmod(base + m, 8)
                factor0 = repeat_row(first[group], row)
                factor1 = repeat_row(second_low[group], row)
                for g in columns[m]:
                    if m < k + 4:
                        step = (second_low[g] * factor1) * inverse1
                        columns[m][g] = (columns[m][g] - multiple0[g] * factor0) - step
                    else:
                        step = multiple0[g] * factor0 + multiple1[g] * factor1
                        columns[m][g] = columns[m][g] - step
            for t in range(len(tiles[own])):
                for multiple, row in ((multiple0, at), (multiple1, at + 1)):
                    factor = repeat_row(tiles[own][t], row)
                    for g in below:
                        tiles[g][t] = tiles[g][t] - multiple[g] * factor
    return pivots


def inverse_factor(schur, size):
    groups, panels = PANEL // 8, size // PANEL
    sub = lax.broadcasted_iota(jnp.int32, (8, 128), 0)
    eye = (
        lax.broadcasted_iota(jnp.int32, (PANEL, PANEL), 0)
        == lax.broadcasted_iota(jnp.int32, (PANEL, PANEL), 1)
    ).astype(F32)
    schur = [schur[i * PANEL : (i + 1) * PANEL, :] for i in range(panels)]
    inverse = [None] * panels
    result = []
    for t in range(panels):
        start = t * PANEL
        lane0 = start // 128 * 128
        left = schur[t][:, lane0:]
        right = [inverse[t]] if t else []
        right.append(eye)
        width = start + PANEL
        if width % 128:
            right.append(jnp.zeros((PANEL, -width % 128), F32))
        right = jnp.concatenate(right, axis=1)
        nl, nr = left.shape[1] // 128, right.shape[1] // 128
        tiles = [
            [left[8 * g : 8 * g + 8, 128 * k : 128 * k + 128] for k in range(nl)]
            + [right[8 * g : 8 * g + 8, 128 * k : 128 * k + 128] for k in range(nr)]
            for g in range(groups)
        ]
        inverses = eliminate(tiles, start - lane0, sub)
        scale = []
        for g in range(groups):
            column = inverses[8 * g]
            for o in range(1, 8):
                column = jnp.where(sub == o, inverses[8 * g + o], column)
            scale.append(column)
        root = [jnp.sqrt(column) for column in scale]
        blank = [jnp.zeros((8, 128), F32)] * (size // 128 - nr)
        result.append(
            jnp.concatenate(
                [
                    jnp.concatenate([tiles[g][nl + k] * root[g] for k in range(nr)] + blank, axis=1)
                    for g in range(groups)
                ],
                axis=0,
            )
        )
        if t == panels - 1:
            break
        upper = jnp.concatenate([jnp.concatenate(tiles[g], axis=1) for g in range(groups)], axis=0)
        scaled = jnp.concatenate(
            [
                jnp.concatenate([tiles[g][k] * scale[g] for k in range(nl)], axis=1)
                for g in range(groups)
            ],
            axis=0,
        )
        for low, high in ((t + 1, t + 2), (t + 2, panels)):
            if low >= high:
                continue
            update = exact_outer(scaled[:, low * PANEL - lane0 : high * PANEL - lane0], upper)
            for i in range(low, high):
                part = update[(i - low) * PANEL : (i - low + 1) * PANEL]
                kept = [schur[i][:, :lane0]] if lane0 else []
                schur[i] = jnp.concatenate(kept + [schur[i][:, lane0:] - part[:, : nl * 128]], axis=1)
                fresh = -part[:, nl * 128 : nl * 128 + width]
                if inverse[i] is not None:
                    fresh = jnp.concatenate([inverse[i] + fresh[:, :start], fresh[:, start:]], axis=1)
                inverse[i] = fresh
    return jnp.concatenate(result, axis=0)


def whiten_kernel(moments_ref, state_ref, out_ref):
    total = moments_ref[...]
    row = lax.broadcasted_iota(jnp.int32, (TARGETS, TARGETS), 0)
    column = lax.broadcasted_iota(jnp.int32, (TARGETS, TARGETS), 1)
    share = 1.0 / total[1:2, 3:4]
    first = jnp.where(column[0:1] == 0, total[1:2, 2:3], total[0:1, :])
    mean = first * share
    outer = lax.dot_general(
        mean, mean, (((0,), (0,)), ((), ())), precision=EXACT, preferred_element_type=F32
    )
    lower = jnp.where(column <= row, total, 0.0)
    strict = jnp.where(column < row, total, 0.0)
    covariance = (lower + strict.T) * share - outer
    covariance = covariance + jnp.where(row == column, SHRINKAGE, 0.0)
    inverse = inverse_factor(covariance, TARGETS)
    profile, _, _, weight = unpack(state_ref[...])
    centered = split((profile - mean) * jnp.sqrt(weight))
    inverse = split(inverse)

    def product(a, b):
        return lax.dot_general(a, b, (((1,), (1,)), ((), ())), preferred_element_type=F32)

    cross = product(centered[0], inverse[1]) + product(centered[1], inverse[0])
    out_ref[...] = product(centered[0], inverse[0]) + cross


def whiten(moments, state):
    return pl.pallas_call(
        whiten_kernel,
        in_specs=[VMEM, VMEM],
        out_specs=VMEM,
        out_shape=jax.ShapeDtypeStruct((state.shape[0], TARGETS), F32),
        compiler_params=params(),
        name="whiten",
    )(moments, state)


def all_sum(moments):
    plane, line = lax.axis_size(PLANE), lax.axis_size("z")
    rows = TARGETS // plane
    parts = lax.all_to_all(moments.reshape(plane, rows, TARGETS), PLANE, 0, 0)
    part = jnp.sum(parts, axis=0, keepdims=True)
    parts = lax.all_to_all(jnp.broadcast_to(part, (line, rows, TARGETS)), "z", 0, 0)
    part = jnp.sum(parts, axis=0, keepdims=True)
    parts = lax.all_to_all(jnp.broadcast_to(part, (plane, rows, TARGETS)), PLANE, 0, 0)
    return parts.reshape(TARGETS, TARGETS)


def on_device(compounds, compound_weight, reference_prints, potency, target_label):
    core = lax.axis_index("core").astype(jnp.int32).reshape(1)
    marks = target_label.astype(F32) * 16.0 + potency.astype(F32)
    mine, other = prepare(core, reference_prints, marks[None, :])

    hold = lax.optimization_barrier
    beside, flipped, rest = send(mine, onward), send(mine, flip), send(other, onward)
    far, flipped_far = send(beside, onward), send(beside, across)
    ahead, ahead_rest = send(flipped, onward), send(rest, flip)
    near = [beside, flipped, rest]
    near += [send(piece, sibling) for piece in near]
    state = first_part(compounds, compound_weight, [mine, other] + near)
    far, flipped_far, ahead, ahead_rest, state = hold((far, flipped_far, ahead, ahead_rest, state))
    last = [far, flipped_far, ahead, ahead_rest]
    others = [send(piece, sibling) for piece in last]
    state = more_part(compounds, state, last)
    state, moments = last_part(compounds, state, others)
    return whiten(all_sum(moments), state)


def solution(mesh):
    sizes = dict(core=2, x_lo=2, x_hi=2)
    sizes["z"] = mesh.shape["lib"] // (sizes["core"] * sizes["x_lo"])
    sizes["y"] = mesh.shape["ref"] // sizes["x_hi"]
    fine = jax.sharding.Mesh(mesh.devices.reshape([sizes[name] for name in ALL]), ALL)
    spread = ALL
    across_refs = ("y", "x_hi")
    placed = (P(spread, None), P(spread), P(across_refs, None), P(across_refs), P(across_refs))
    return jax.shard_map(
        on_device, mesh=fine, in_specs=placed, out_specs=P(spread, None), check_vma=False
    )
```

```python
import functools

import jax
import jax.numpy as jnp
from jax import lax
from jax.experimental import pallas as pl
from jax.experimental.pallas import tpu as pltpu
from jax.sharding import PartitionSpec as P

ALL = ("z", "x_lo", "core", "y", "x_hi")
PLANE = ("x_lo", "core", "y", "x_hi")
BITS = 512
EXTRA = 16
DEPTH = BITS + EXTRA
TARGETS = 256
SHRINKAGE = 0.02
LOG2E = 1.4426950408889634
SCALE = 320.0 * LOG2E
MARGIN = 58.0
PANEL = 32
SPREAD = 16
REDO = 128
F32 = jnp.float32
BF16 = jnp.bfloat16
VMEM = pl.BlockSpec(memory_space=pltpu.VMEM)


def params(mib=20):
    return pltpu.CompilerParams(vmem_limit_bytes=mib * 2**20)


def cost(flops, size):
    return pl.CostEstimate(flops=flops, bytes_accessed=size, transcendentals=0)


def place(x, y, z, c):
    return ((z % 8 * 2 + x % 2) * 2 + c % 2) * 8 + y % 4 * 2 + x // 2


def route(move):
    pairs = []
    for x in range(4):
        for y in range(4):
            for z in range(8):
                for c in range(2):
                    pairs.append((place(x, y, z, c), place(*move(x, y, z, c))))
    return sorted(pairs)


def send(value, move):
    return lax.ppermute(value, ALL, route(move))


def flip(x, y, z, c):
    return 3 - x, y, z, c


def onward(x, y, z, c):
    return x, y + 1 - 2 * c, z, c


def across(x, y, z, c):
    return 3 - x, y + 1 - 2 * c, z, c


def sibling(x, y, z, c):
    return x, y, z, 1 - c


def prep_kernel(core_ref, prints_ref, marks_ref, mine_ref, other_ref):
    prints = prints_ref[...].T
    wide = prints.astype(F32)
    norm = jnp.sum(wide * wide, axis=0, keepdims=True)
    high = norm.astype(BF16)
    rest = norm - high.astype(F32)
    middle = rest.astype(BF16)
    low = (rest - middle.astype(F32)).astype(BF16)
    marks = marks_ref[...]
    label = jnp.floor(marks * (1.0 / 16.0))
    row = lax.broadcasted_iota(jnp.int32, (EXTRA, prints.shape[1]), 0)
    extra = jnp.where(row == 0, marks - 16.0 * label, 0.0)
    extra = jnp.where(row == 1, label, extra)
    for at, part in ((2, high), (3, middle), (4, low)):
        extra = jnp.where(row == at, part.astype(F32), extra)
    extra = extra.astype(BF16)
    half = prints.shape[1] // 2

    def store(mine, other):
        for ref, part in ((mine_ref, mine), (other_ref, other)):
            ref[:BITS, :] = prints[:, part]
            ref[BITS:, :] = extra[:, part]

    @pl.when(core_ref[0] == 0)
    def _():
        store(slice(0, half), slice(half, None))

    @pl.when(core_ref[0] != 0)
    def _():
        store(slice(half, None), slice(0, half))


def prepare(core, prints, marks):
    shape = jax.ShapeDtypeStruct((DEPTH, prints.shape[0] // 2), BF16)
    return pl.pallas_call(
        prep_kernel,
        in_specs=[pl.BlockSpec(memory_space=pltpu.SMEM), VMEM, VMEM],
        out_specs=[VMEM, VMEM],
        out_shape=[shape, shape],
        compiler_params=params(),
        name="prepare",
    )(core, prints, marks)


def piece_scores(queries, query_norm, piece_ref):
    extra = piece_ref[BITS:, :].astype(F32)
    norm = extra[2:3] + extra[3:4] + extra[4:5]
    inter = jnp.dot(queries, piece_ref[:BITS, :], preferred_element_type=F32)
    inverse = 1.0 / ((query_norm + norm) - inter)
    return (inter * inverse) * SCALE


def piece_values(piece_ref):
    extra = piece_ref[BITS:, :].astype(F32)
    target = lax.broadcasted_iota(jnp.int32, (TARGETS, extra.shape[1]), 0)
    hit = target == extra[1:2].astype(jnp.int32)
    return jnp.where(hit, extra[0:1], 0.0).astype(BF16)


def add_piece(scores, top, piece_ref, num, den):
    expo = jnp.exp2(scores - top).astype(BF16)
    rounded = expo.astype(F32)
    for k in range(expo.shape[1] // 128):
        den = den + rounded[:, k * 128 : (k + 1) * 128]
    num = num + lax.dot_general(
        expo,
        piece_values(piece_ref),
        (((1,), (1,)), ((), ())),
        preferred_element_type=F32,
    )
    return num, den


def squared_norm(queries):
    wide = queries.astype(F32)
    return jnp.sum(wide * wide, axis=1, keepdims=True)


def unpack(state):
    num, marks = state[:, :TARGETS], state[:, TARGETS:]
    lane = lax.broadcasted_iota(jnp.int32, marks.shape, 1)
    return num, jnp.where(lane == 1, marks, 0.0), marks[:, 0:1], marks[:, 2:3]


def pack(num, den, top, weight):
    lane = lax.broadcasted_iota(jnp.int32, den.shape, 1)
    marks = jnp.where(lane == 0, top, jnp.sum(den, axis=1, keepdims=True))
    marks = jnp.where(lane == 2, weight, marks)
    return jnp.concatenate([num, marks], axis=1)


def empty(rows):
    return jnp.zeros((rows, TARGETS), F32), jnp.zeros((rows, 128), F32)


def add_pieces(queries_ref, state_in, state_ref, pieces, weight=None):
    queries = queries_ref[...]
    query_norm = squared_norm(queries)
    if state_in is None:
        num, den = empty(queries.shape[0])
        top = None
    else:
        num, den, top, weight = unpack(state_in[...])
    for piece_ref in pieces:
        scores = piece_scores(queries, query_norm, piece_ref)
        if top is None:
            top = jnp.max(scores, axis=1, keepdims=True) + MARGIN
        num, den = add_piece(scores, top, piece_ref, num, den)
    fits = jnp.max(den) <= 1.0

    @pl.when(fits)
    def _():
        state_ref[...] = pack(num, den, top, weight)

    @pl.when(jnp.logical_not(fits))
    def _():
        if state_in is None:
            state_ref[...] = pack(num, den, top, weight)

        @pl.loop(0, queries_ref.shape[0] // REDO)
        def _(block):
            here = pl.ds(pl.multiple_of(block * REDO, REDO), REDO)
            queries = queries_ref[here, :]
            query_norm = squared_norm(queries)
            best = jnp.zeros((REDO, 1), F32)
            for piece_ref in pieces:
                scores = piece_scores(queries, query_norm, piece_ref)
                best = jnp.maximum(best, jnp.max(scores, axis=1, keepdims=True))
            if state_in is None:
                top = best + MARGIN
                num, den = empty(REDO)
                weight = unpack(state_ref[here, :])[3]
            else:
                num, den, old, weight = unpack(state_in[here, :])
                top = jnp.maximum(old, best + MARGIN)
                scale = jnp.exp2(old - top)
                num, den = num * scale, den * scale
            for piece_ref in pieces:
                scores = piece_scores(queries, query_norm, piece_ref)
                num, den = add_piece(scores, top, piece_ref, num, den)
            state_ref[here, :] = pack(num, den, top, weight)


def first_kernel(queries_ref, weight_ref, *refs):
    columns = weight_ref[...].T
    weight = jnp.concatenate([columns[:, k : k + 1] for k in range(columns.shape[1])], axis=0)
    add_pieces(queries_ref, None, refs[-1], refs[:-1], weight)


def more_kernel(queries_ref, state_in, *refs):
    add_pieces(queries_ref, state_in, refs[-1], refs[:-1])


def split(value):
    high = value.astype(BF16)
    return high, (value - high.astype(F32)).astype(BF16)


def last_kernel(count, queries_ref, state_in, *refs):
    state_ref, moments_ref = refs[count:]
    add_pieces(queries_ref, state_in, state_ref, refs[:count])
    num, den, _, weight = unpack(state_ref[...])
    profile = num * (1.0 / jnp.sum(den, axis=1, keepdims=True))
    state_ref[:, :TARGETS] = profile
    weight_total = jnp.sum(weight, axis=0, keepdims=True)
    first = jnp.sum(profile * weight, axis=0, keepdims=True)
    mean = first / weight_total
    spread = (profile - mean) * jnp.sqrt(weight)
    outer = (((0,), (0,)), ((), ()))
    high, low = split(spread)
    cross = lax.dot_general(high, low, outer, preferred_element_type=F32)
    moments = lax.dot_general(high, high, outer, preferred_element_type=F32) + (cross + cross.T)
    moments = moments + jnp.broadcast_to(mean, (TARGETS, TARGETS)).T * first
    row = lax.broadcasted_iota(jnp.int32, (TARGETS, TARGETS), 0)
    column = lax.broadcasted_iota(jnp.int32, (TARGETS, TARGETS), 1)
    moments = jnp.where((row == 0) & (column > 0), first, moments)
    moments = jnp.where((row == 1) & (column == 2), first[0:1, 0:1], moments)
    moments = jnp.where((row == 1) & (column == 3), weight_total, moments)
    moments_ref[...] = moments


def work(rows, pieces):
    refs = sum(piece.shape[1] for piece in pieces)
    return cost(6 * rows * refs * (BITS + TARGETS), rows * 2048 + refs * DEPTH * 2)


def state_shape(rows):
    return jax.ShapeDtypeStruct((rows, TARGETS + 128), F32)


def first_part(queries, weight, pieces):
    rows = queries.shape[0]
    return pl.pallas_call(
        first_kernel,
        in_specs=[VMEM] * (2 + len(pieces)),
        out_specs=VMEM,
        out_shape=state_shape(rows),
        compiler_params=params(),
        cost_estimate=work(rows, pieces),
        name="first_part",
    )(queries, weight.reshape(rows // 128, 128), *pieces)


def more_part(queries, state, pieces):
    rows = queries.shape[0]
    return pl.pallas_call(
        more_kernel,
        in_specs=[VMEM] * (2 + len(pieces)),
        out_specs=VMEM,
        out_shape=state_shape(rows),
        input_output_aliases={1: 0},
        compiler_params=params(),
        cost_estimate=work(rows, pieces),
        name="more_part",
    )(queries, state, *pieces)


def last_part(queries, state, pieces):
    rows = queries.shape[0]
    return pl.pallas_call(
        functools.partial(last_kernel, len(pieces)),
        in_specs=[VMEM] * (2 + len(pieces)),
        out_specs=[VMEM] * 2,
        out_shape=[state_shape(rows), jax.ShapeDtypeStruct((TARGETS, TARGETS), F32)],
        input_output_aliases={1: 0},
        compiler_params=params(),
        cost_estimate=work(rows, pieces),
        name="last_part",
    )(queries, state, *pieces)


def repeat_row(block, at):
    return jnp.broadcast_to(block[at : at + 1, :], block.shape)


def three_way(value):
    high = value.astype(BF16)
    rest = value - high.astype(F32)
    middle = rest.astype(BF16)
    return high, middle, (rest - middle.astype(F32)).astype(BF16)


def exact_outer(a, b):
    a0, a1, a2 = three_way(a)
    b0, b1, b2 = three_way(b)
    left = jnp.concatenate([a2, a0, a1, a1, a0, a0], axis=0)
    right = jnp.concatenate([b0, b2, b1, b0, b1, b0], axis=0)
    return lax.dot_general(left, right, (((0,), (0,)), ((), ())), preferred_element_type=F32)


def eliminate(tiles, square, sub):
    groups, pivots = len(tiles), []
    at_tile, at_lane = divmod(square, 128)
    for base in range(0, PANEL, SPREAD):
        columns = [
            {
                g: jnp.broadcast_to(tiles[g][at_tile][:, lane : lane + 1], (8, 128))
                for g in range((base + k) // 8, groups)
            }
            for k, lane in enumerate(range(at_lane + base, at_lane + base + SPREAD))
        ]
        for k in range(0, SPREAD, 2):
            own, at = divmod(base + k, 8)
            first, second = columns[k], columns[k + 1]
            a, b = repeat_row(first[own], at), repeat_row(first[own], at + 1)
            c = repeat_row(second[own], at + 1)
            inverse0 = 1.0 / a
            inverse1 = a * (1.0 / (a * c - b * b))
            pivots += [inverse0, inverse1]
            below = range(own, groups)
            first_low = {g: jnp.where(sub > at, first[g], 0.0) if g == own else first[g] for g in below}
            multiple0 = {g: first_low[g] * inverse0 for g in below}
            second_low = {g: second[g] - multiple0[g] * b for g in below}
            second_low[own] = jnp.where(sub > at + 1, second_low[own], 0.0)
            multiple1 = {g: second_low[g] * inverse1 for g in below}
            for m in range(k + 2, SPREAD):
                group, row = divmod(base + m, 8)
                factor0 = repeat_row(first[group], row)
                factor1 = repeat_row(second_low[group], row)
                for g in columns[m]:
                    if m < k + 4:
                        step = (second_low[g] * factor1) * inverse1
                        columns[m][g] = (columns[m][g] - multiple0[g] * factor0) - step
                    else:
                        step = multiple0[g] * factor0 + multiple1[g] * factor1
                        columns[m][g] = columns[m][g] - step
            for t in range(len(tiles[own])):
                for multiple, row in ((multiple0, at), (multiple1, at + 1)):
                    factor = repeat_row(tiles[own][t], row)
                    for g in below:
                        tiles[g][t] = tiles[g][t] - multiple[g] * factor
    return pivots


def inverse_factor(schur, size):
    groups, panels = PANEL // 8, size // PANEL
    sub = lax.broadcasted_iota(jnp.int32, (8, 128), 0)
    eye = (
        lax.broadcasted_iota(jnp.int32, (PANEL, PANEL), 0)
        == lax.broadcasted_iota(jnp.int32, (PANEL, PANEL), 1)
    ).astype(F32)
    schur = [schur[i * PANEL : (i + 1) * PANEL, :] for i in range(panels)]
    inverse = [None] * panels
    result = []
    for t in range(panels):
        start = t * PANEL
        lane0 = start // 128 * 128
        left = schur[t][:, lane0:]
        right = [inverse[t]] if t else []
        right.append(eye)
        width = start + PANEL
        if width % 128:
            right.append(jnp.zeros((PANEL, -width % 128), F32))
        right = jnp.concatenate(right, axis=1)
        nl, nr = left.shape[1] // 128, right.shape[1] // 128
        tiles = [
            [left[8 * g : 8 * g + 8, 128 * k : 128 * k + 128] for k in range(nl)]
            + [right[8 * g : 8 * g + 8, 128 * k : 128 * k + 128] for k in range(nr)]
            for g in range(groups)
        ]
        inverses = eliminate(tiles, start - lane0, sub)
        scale = []
        for g in range(groups):
            column = inverses[8 * g]
            for o in range(1, 8):
                column = jnp.where(sub == o, inverses[8 * g + o], column)
            scale.append(column)
        root = [jnp.sqrt(column) for column in scale]
        blank = [jnp.zeros((8, 128), F32)] * (size // 128 - nr)
        result.append(
            jnp.concatenate(
                [
                    jnp.concatenate([tiles[g][nl + k] * root[g] for k in range(nr)] + blank, axis=1)
                    for g in range(groups)
                ],
                axis=0,
            )
        )
        if t == panels - 1:
            break
        upper = jnp.concatenate([jnp.concatenate(tiles[g], axis=1) for g in range(groups)], axis=0)
        scaled = jnp.concatenate(
            [
                jnp.concatenate([tiles[g][k] * scale[g] for k in range(nl)], axis=1)
                for g in range(groups)
            ],
            axis=0,
        )
        for low, high in ((t + 1, t + 2), (t + 2, panels)):
            if low >= high:
                continue
            update = exact_outer(scaled[:, low * PANEL - lane0 : high * PANEL - lane0], upper)
            for i in range(low, high):
                part = update[(i - low) * PANEL : (i - low + 1) * PANEL]
                kept = [schur[i][:, :lane0]] if lane0 else []
                schur[i] = jnp.concatenate(kept + [schur[i][:, lane0:] - part[:, : nl * 128]], axis=1)
                fresh = -part[:, nl * 128 : nl * 128 + width]
                if inverse[i] is not None:
                    fresh = jnp.concatenate([inverse[i] + fresh[:, :start], fresh[:, start:]], axis=1)
                inverse[i] = fresh
    return jnp.concatenate(result, axis=0)


def whiten_kernel(moments_ref, state_ref, out_ref):
    total = moments_ref[...]
    row = lax.broadcasted_iota(jnp.int32, (TARGETS, TARGETS), 0)
    column = lax.broadcasted_iota(jnp.int32, (TARGETS, TARGETS), 1)
    share = 1.0 / total[1:2, 3:4]
    first = jnp.where(column[0:1] == 0, total[1:2, 2:3], total[0:1, :])
    mean = first * share
    outer = jnp.broadcast_to(mean, (TARGETS, TARGETS)).T * mean
    lower = jnp.where(column <= row, total, 0.0)
    strict = jnp.where(column < row, total, 0.0)
    covariance = (lower + strict.T) * share - outer
    covariance = covariance + jnp.where(row == column, SHRINKAGE, 0.0)
    inverse = inverse_factor(covariance, TARGETS)
    profile, _, _, weight = unpack(state_ref[...])
    centered = split((profile - mean) * jnp.sqrt(weight))
    inverse = split(inverse)

    def product(a, b):
        return lax.dot_general(a, b, (((1,), (1,)), ((), ())), preferred_element_type=F32)

    cross = product(centered[0], inverse[1]) + product(centered[1], inverse[0])
    out_ref[...] = product(centered[0], inverse[0]) + cross


def whiten(moments, state):
    return pl.pallas_call(
        whiten_kernel,
        in_specs=[VMEM, VMEM],
        out_specs=VMEM,
        out_shape=jax.ShapeDtypeStruct((state.shape[0], TARGETS), F32),
        compiler_params=params(),
        name="whiten",
    )(moments, state)


def all_sum(moments):
    plane, line = lax.axis_size(PLANE), lax.axis_size("z")
    rows = TARGETS // plane
    parts = lax.all_to_all(moments.reshape(plane, rows, TARGETS), PLANE, 0, 0)
    part = jnp.sum(parts, axis=0, keepdims=True)
    parts = lax.all_to_all(jnp.broadcast_to(part, (line, rows, TARGETS)), "z", 0, 0)
    part = jnp.sum(parts, axis=0, keepdims=True)
    parts = lax.all_to_all(jnp.broadcast_to(part, (plane, rows, TARGETS)), PLANE, 0, 0)
    return parts.reshape(TARGETS, TARGETS)


def on_device(compounds, compound_weight, reference_prints, potency, target_label):
    core = lax.axis_index("core").astype(jnp.int32).reshape(1)
    marks = target_label.astype(F32) * 16.0 + potency.astype(F32)
    mine, other = prepare(core, reference_prints, marks[None, :])

    hold = lax.optimization_barrier
    beside, flipped, rest = send(mine, onward), send(mine, flip), send(other, onward)
    far, flipped_far = send(beside, onward), send(beside, across)
    ahead, ahead_rest = send(flipped, onward), send(rest, flip)
    near = [beside, flipped, rest]
    near += [send(piece, sibling) for piece in near]
    state = first_part(compounds, compound_weight, [mine, other] + near)
    far, flipped_far, ahead, ahead_rest, state = hold((far, flipped_far, ahead, ahead_rest, state))
    last = [far, flipped_far, ahead, ahead_rest]
    others = [send(piece, sibling) for piece in last]
    state = more_part(compounds, state, last)
    state, moments = last_part(compounds, state, others)
    return whiten(all_sum(moments), state)


def solution(mesh):
    sizes = dict(core=2, x_lo=2, x_hi=2)
    sizes["z"] = mesh.shape["lib"] // (sizes["core"] * sizes["x_lo"])
    sizes["y"] = mesh.shape["ref"] // sizes["x_hi"]
    fine = jax.sharding.Mesh(mesh.devices.reshape([sizes[name] for name in ALL]), ALL)
    spread = ALL
    across_refs = ("y", "x_hi")
    placed = (P(spread, None), P(spread), P(across_refs, None), P(across_refs), P(across_refs))
    return jax.shard_map(
        on_device, mesh=fine, in_specs=placed, out_specs=P(spread, None), check_vma=False
    )
```
